768 devices in a mesh: blk: 96 (over x, y_lo, z), dp: 8 (over y_hi, core).
Axes of the slice: x: 4, y: 8 (y_hi: 4, y_lo: 2; y = y_hi * 2 + y_lo), z: 12, core: 2. Of those that a mesh axis runs over, the one named last changes fastest.
Arguments:
- image_emb: bfloat16 [196608, 1152], P(('blk', 'dp')), may hold values from -0.1875 to 0.1875
- text_feat: bfloat16 [196608, 1152], P(('blk', 'dp')), may hold values from -0.1875 to 0.1875
- text_proj: bfloat16 [1152, 1152], P('dp'), may hold values from -0.1875 to 0.1875
- pos_index: int32 [768, 256], P(('blk', 'dp')), may hold values from 0 to 255, each once within a row
- scale: float32 [1], replicated, may hold values from 4 to 8
- bias: float32 [1], replicated, may hold values from -2 to 0
Outputs:
- grad_image: float32 [196608, 1152], P(('blk', 'dp'))
- grad_text_feat: float32 [196608, 1152], P(('blk', 'dp'))
- grad_proj: float32 [1152, 1152], P('dp')
The draws below stay inside these ranges and needn't reach their ends.
Inputs may be any that keep to these rules, and one draw needn't show every extreme that they name: Each row of pos_index is a permutation of 0 to 255.
All inputs are finite; a program needn't handle non-finite values.
Results may differ from the reference program's by a relative error of at most 0.0053.
Values may be sent and summed in bfloat16 or wider, within the bound.
A program may use at most 64 MiB of HBM per device.

```python
import jax
import jax.numpy as jnp
from jax import lax

D = 1152
ROWS = 256
GROUPS = 768
BATCH = 196608
N_BLK = 96
N_DP = 8


def level_of(rng, dims, shards, least, top_value):
    def one(axis_at, shards_of):
        steps = jax.random.uniform(jax.random.fold_in(jax.random.fold_in(rng, 6), axis_at), (shards_of,), jnp.float32, least / len(shards), top_value / len(shards))
        return jnp.repeat(jnp.exp(steps), dims[axis_at] // shards_of).reshape((-1,) + (1,) * (len(dims) - axis_at - 1))

    factor_of = one(*shards[0])
    for cut in shards[1:]:
        factor_of = factor_of * one(*cut)
    return factor_of


def bell_draw(own_key, extent, width, limit, shards=(), held_as=jnp.bfloat16):
    gain = level_of(own_key, extent, shards, -0.22, 0.18) if shards else 1.0
    values = jax.random.normal(own_key, extent, jnp.float32) * width * gain
    return jnp.minimum(jnp.maximum(values, -limit), limit).astype(held_as)


def setup_inputs(seed: int = 0) -> dict:
    streams_of = jax.random.split(jax.random.key(seed), 7)
    return {
        "image_emb": bell_draw(streams_of[0], (BATCH, D), (D ** -0.5), 0.1875, ((0, 768),)),
        "text_feat": bell_draw(streams_of[1], (BATCH, D), (D ** -0.5), 0.1875, ((0, 768),)),
        "text_proj": bell_draw(streams_of[2], (D, D), D ** -0.5, 0.1875, ((0, 8),)),
        "pos_index": jax.vmap(lambda own: jax.random.permutation(own, ROWS))(jax.random.split(streams_of[3], GROUPS)).reshape((GROUPS, ROWS)).astype(jnp.int32),
        "scale": jnp.clip(jax.random.uniform(streams_of[4], (1,), jnp.float32, 4.0, 8.0), 4.0, 8.0),
        "bias": jnp.clip(jax.random.uniform(streams_of[5], (1,), jnp.float32, -2.0, 0.0), -2.0, 0.0),
    }


def row_norm(values):
    return jnp.sqrt(lax.optimization_barrier(jnp.sum(values * values, axis=-1, keepdims=True)) + 1e-06)

def norm_back(values, norms, grads):
    inner = lax.optimization_barrier(jnp.sum(values * grads, axis=-1, keepdims=True))
    return grads / norms - values * inner / (norms * norms * norms)

def reference(image_emb, text_feat, text_proj, pos_index, scale, bias):
    text_emb = jnp.dot(text_feat, text_proj, preferred_element_type=jnp.float32)
    image_f = image_emb.astype(jnp.float32)
    image_norm = row_norm(image_f)
    text_norm = row_norm(text_emb)
    image_unit = (image_f / image_norm).astype(jnp.bfloat16)
    text_unit = (text_emb / text_norm).astype(jnp.bfloat16)
    shape4 = (N_BLK, N_DP, ROWS, D)
    image4 = image_unit.reshape(shape4).astype(jnp.float32)
    text4 = text_unit.reshape(shape4).astype(jnp.float32)
    prev4 = jnp.roll(text4, 1, axis=0)
    factor = scale[0]
    offset = bias[0]
    own_logit = factor * jnp.einsum('bgrd,bgcd->bgrc', image4, text4) + offset
    near_logit = factor * jnp.einsum('bgrd,bgcd->bgrc', image4, prev4) + offset
    positions = pos_index.reshape(N_BLK, N_DP, ROWS)
    columns = jnp.arange(ROWS, dtype=jnp.int32)
    label = jnp.where(columns[None, None, None, :] == positions[..., None], 1.0, -1.0).astype(jnp.float32)
    own_coef = (-label * jax.nn.sigmoid(-label * own_logit)).astype(jnp.bfloat16).astype(jnp.float32)
    near_coef = jax.nn.sigmoid(near_logit).astype(jnp.bfloat16).astype(jnp.float32)
    grad_iu = factor * jnp.einsum('bgrc,bgcd->bgrd', own_coef, text4) + factor * jnp.einsum('bgrc,bgcd->bgrd', near_coef, prev4)
    near_text = factor * jnp.einsum('bgrc,bgrd->bgcd', near_coef, image4)
    grad_tu = factor * jnp.einsum('bgrc,bgrd->bgcd', own_coef, image4) + jnp.roll(near_text, -1, axis=0)
    grad_iu = grad_iu.reshape(BATCH, D)
    grad_tu = grad_tu.reshape(BATCH, D)
    grad_image = norm_back(image_f, image_norm, grad_iu)
    grad_te = norm_back(text_emb, text_norm, grad_tu).astype(jnp.bfloat16)
    grad_text_feat = jnp.dot(grad_te, text_proj.T, preferred_element_type=jnp.float32)
    grad_proj = jnp.dot(text_feat.T, grad_te, preferred_element_type=jnp.float32)
    return (grad_image, grad_text_feat, grad_proj)
```

```python
import jax
import jax.numpy as jnp
from jax import lax
from jax.experimental import pallas as pl
from jax.experimental.pallas import tpu as pltpu
from jax.sharding import PartitionSpec as P

MESH = pl.DeviceIdType.MESH
BF = jnp.bfloat16
F32 = jnp.float32
NX, NY, NZ, NH = 4, 8, 12, 4
ROWS, D, SH = 256, 1152, 144
PART = 32
UA, UB = 7, 4
UN = UA + UB
TILES = 81
COLS = 384
IMG = 2


def place():
    b, d = lax.axis_index("blk"), lax.axis_index("dp")
    x = b // (2 * NZ)
    low = lax.rem(b // NZ, 2)
    z = lax.rem(b, NZ)
    return b, d, x, (d // 2) * 2 + low, z, lax.rem(d, 2)


def device(x, y, z, c):
    return (x * (2 * NZ) + lax.rem(y, 2) * NZ + z, (y // 2) * 2 + c)


def nt_dot(a, b):
    return lax.dot_general(a, b, (((1,), (1,)), ((), ())), preferred_element_type=F32)


def nn_dot(a, b):
    return jnp.dot(a, b, preferred_element_type=F32)


def sigmoid(v):
    return 1.0 / (1.0 + jnp.exp(-v))


def inv_norm(v):
    return lax.rsqrt(jnp.sum(v * v, axis=-1, keepdims=True) + 1e-06)


def unit_rows(src, unit, inv, step=64):
    def body(i, _):
        rows = pl.ds(pl.multiple_of(i * step, step), step)
        v = src[rows].astype(F32)
        r = inv_norm(v)
        unit[rows] = (v * r).astype(BF)
        if inv is not None:
            inv[rows] = r
        return 0

    lax.fori_loop(0, src.shape[0] // step, body, 0)


def norm_back(src, inv, grad, out, step=64):
    def body(i, _):
        rows = pl.ds(pl.multiple_of(i * step, step), step)
        v, r, g = src[rows].astype(F32), inv[rows], grad[rows]
        inner = jnp.sum(v * g, axis=-1, keepdims=True)
        out[rows] = (r * (g - v * (inner * r * r))).astype(out.dtype)
        return 0

    lax.fori_loop(0, src.shape[0] // step, body, 0)


def by_columns(fn):
    def body(i, _):
        fn(pl.ds(pl.multiple_of(i * COLS, COLS), COLS))
        return 0

    lax.fori_loop(0, D // COLS, body, 0)


def kernel(
    image, feat, proj, pos, scale, bias,
    g_image, g_feat, g_proj,
    full, image_n, feat_p, tft, tft_o, unit_i, unit_n, unit_t, unit_p, inv_i, inv_t, inv_p,
    text, text_p, acc_t, acc_i, gte, gte_o, part, send_a, send_b, got_a, got_b,
    mid_a, mid_b, got_a2, got_b2, zin, got_z, fin,
    s_img, r_img, s_txt, r_txt, s_py, r_py, s_pt, r_pt, s_px, r_px, s_pc, r_pc,
    s_tf, r_tf, s_ge, r_ge, s_a, r_a, s_b, r_b, s_a2, r_a2, s_b2, r_b2,
    s_z, r_z, s_gz, r_gz, s_gx, r_gx, s_gy, r_gy,
):
    b, d, x, y, z, c = place()
    n_blk = lax.axis_size("blk")
    h, low = y // 2, lax.rem(y, 2)
    prev = (lax.rem(b + n_blk - 1, n_blk), d)
    nxt = (lax.rem(b + 1, n_blk), d)
    mate = device(x, y, z, 1 - c)
    xs = [lax.rem(x + o, NX) for o in range(NX)]
    ys = [lax.rem(y + o, NY) for o in range(NY)]
    zs = [lax.rem(z + o, NZ) for o in range(NZ)]
    to_x = [device(v, y, z, c) for v in xs]
    to_y = [device(x, v, z, c) for v in ys]
    to_z = [device(x, y, v, c) for v in zs]
    pending = []

    def send(src, dst, s, r, dev):
        cp = pltpu.make_async_remote_copy(
            src_ref=src, dst_ref=dst, send_sem=s, recv_sem=r, device_id=dev, device_id_type=MESH
        )
        cp.start()
        pending.append(cp)
        return cp

    barrier = pltpu.get_barrier_semaphore()
    partners = to_x[1:] + to_y[1:] + to_z[1:] + [mate, prev, nxt]
    for dev in partners:
        pl.semaphore_signal(barrier, inc=1, device_id=dev, device_id_type=MESH)
    pl.semaphore_wait(barrier, len(partners))

    step = ROWS // IMG
    c_img = [
        send(image.at[pl.ds(i * step, step)], image_n.at[pl.ds(i * step, step)], s_img.at[i], r_img.at[i], prev)
        for i in range(IMG)
    ]
    sign = 2 * low - 1
    mine = pl.multiple_of(d * SH, 16)
    xrow = pl.multiple_of(x * PART, 16)
    c_py, c_pt = [], []
    for k in range(3):
        dev = device(x, lax.rem(y + sign * (k + 1) + NY, NY), z, c)
        c_py.append(
            send(
                proj.at[pl.ds(xrow, PART)],
                full.at[pl.ds(pl.multiple_of(mine + xrow, 16), PART)],
                s_py.at[k], r_py.at[k], dev,
            )
        )
    for k in range(3):
        dev = device(x, lax.rem(y + sign * (k + 1) + NY, NY), z, c)
        c_pt.append(
            send(
                proj.at[pl.ds(NX * PART, SH - NX * PART)],
                full.at[pl.ds(pl.multiple_of(mine + NX * PART, 16), SH - NX * PART)],
                s_pt.at[k], r_pt.at[k], dev,
            )
        )
    c_pc = [send(proj, full.at[pl.ds(mine, SH)], s_pc.at[3], r_pc.at[3], mate)]
    c_txt = send(feat, feat_p, s_txt.at[0], r_txt.at[0], nxt)
    full[pl.ds(mine, SH)] = proj[...]

    for i in range(8):
        pass
    turned = feat[...].T
    for i in range(8):
        tft[i // 2, i % 2] = turned[i * SH : (i + 1) * SH]
    c_tf = send(tft.at[:, 1 - c], tft_o, s_tf.at[0], r_tf.at[0], mate)
    unit_rows(image, unit_i, inv_i)

    rows_of = []
    for k, hop in enumerate((1, -2, 3)):
        src_y = lax.rem(y + sign * hop + NY, NY)
        rows_of.append(((src_y // 2) * 2 + c) * SH)
    c_px = []
    for k in range(3):
        c_py[k].wait_recv()
        where = full.at[pl.ds(pl.multiple_of(rows_of[k] + xrow, 16), PART)]
        c_px.append([send(where, where, s_px.at[k, o - 1], r_px.at[k, o - 1], to_x[o]) for o in range(1, NX)])
    for k in range(3):
        c_pt[k].wait_recv()
        for cp in c_px[k]:
            cp.wait_recv()
        where = full.at[pl.ds(pl.multiple_of(rows_of[k], 16), SH)]
        c_pc.append(send(where, where, s_pc.at[k], r_pc.at[k], mate))
    for cp in c_pc:
        cp.wait_recv()

    def text_cols(cols):
        text[:, cols] = nn_dot(feat[...], full[:, cols])

    by_columns(text_cols)
    unit_rows(text, unit_t, inv_t)
    factor = scale[0]
    offset = bias[0]

    logit = factor * nt_dot(unit_t[...], unit_i[...]) + offset
    hit = lax.broadcasted_iota(jnp.int32, (ROWS, ROWS), 0) == pos[...]
    label = jnp.where(hit, 1.0, -1.0).astype(F32)
    coef = -label * sigmoid(-label * logit)
    coef_t = coef.astype(BF)
    coef_i = coef.T.astype(BF)

    def own_cols(cols):
        acc_t[:, cols] = nn_dot(coef_t, unit_i[:, cols])
        acc_i[:, cols] = nn_dot(coef_i, unit_t[:, cols])

    by_columns(own_cols)

    for i in range(IMG):
        c_img[i].wait_recv()
        rows = pl.ds(i * step, step)
        unit_rows(image_n.at[rows], unit_n.at[rows], None)
        near = sigmoid(factor * nt_dot(unit_t[...], unit_n[rows]) + offset).astype(BF)

        def near_cols(cols):
            acc_t[:, cols] += nn_dot(near, unit_n[rows, cols])

        by_columns(near_cols)

    def scaled(i, _):
        rows = pl.ds(pl.multiple_of(i * 64, 64), 64)
        acc_t[rows] = factor * acc_t[rows]
        return 0

    lax.fori_loop(0, ROWS // 64, scaled, 0)
    norm_back(text, inv_t, acc_t, gte)
    c_ge = send(gte, gte_o, s_ge.at[0], r_ge.at[0], mate)

    def first_half(i, _):
        part[i] = nn_dot(tft[i, c], gte[...])
        return 0

    lax.fori_loop(0, NH, first_half, 0)
    c_tf.wait_recv()
    c_ge.wait_recv()

    def second_half(i, _):
        both = (part[i] + nn_dot(tft_o[i], gte_o[...])).astype(BF)
        for t in range(2 * NX * UN):
            l, xo, u = t // (NX * UN), (t // UN) % NX, t % UN
            if t < TILES:
                row, col = (t // 9) * 16, (t % 9) * 128
                tile = both[row : row + 16, col : col + 128]
            else:
                tile = jnp.zeros((16, 128), BF)
            if u < UA:
                send_a[xo, 2 * i + l, u] = tile
            else:
                send_b[2 * i + l, xo, u - UA] = tile
        return 0

    lax.fori_loop(0, NH, second_half, 0)
    c_a = [send(send_a.at[xs[o]], got_a.at[o - 1], s_a.at[o - 1], r_a.at[o - 1], to_x[o]) for o in range(1, NX)]
    c_b = [send(send_b.at[ys[o]], got_b.at[o - 1], s_b.at[o - 1], r_b.at[o - 1], to_y[o]) for o in range(1, NY)]

    def feat_cols(i, _):
        rows = pl.ds(pl.multiple_of(i * 64, 64), 64)
        g_feat[rows] = nt_dot(gte[rows], full[...]).astype(BF)
        return 0

    lax.fori_loop(0, ROWS // 64, feat_cols, 0)
    c_txt.wait_recv()

    def text_p_cols(cols):
        text_p[:, cols] = nn_dot(feat_p[...], full[:, cols])

    by_columns(text_p_cols)
    unit_rows(text_p, unit_p, None)
    near_p = sigmoid(factor * nt_dot(unit_i[...], unit_p[...]) + offset).astype(BF)

    def image_cols(cols):
        acc_i[:, cols] = factor * (acc_i[:, cols] + nn_dot(near_p, unit_p[:, cols]))

    by_columns(image_cols)
    norm_back(image, inv_i, acc_i, g_image)

    for cp in c_a:
        cp.wait_recv()

    def sum_a(i, _):
        v = send_a[x, i].astype(F32)
        for o in range(NX - 1):
            v = v + got_a[o, i].astype(F32)
        mid_a[i] = v.astype(BF)
        return 0

    lax.fori_loop(0, NY, sum_a, 0)
    c_a2 = [send(mid_a.at[ys[o]], got_a2.at[o - 1], s_a2.at[o - 1], r_a2.at[o - 1], to_y[o]) for o in range(1, NY)]
    for cp in c_b:
        cp.wait_recv()

    def sum_b(i, _):
        v = send_b[y, i].astype(F32)
        for o in range(NY - 1):
            v = v + got_b[o, i].astype(F32)
        mid_b[i] = v.astype(BF)
        return 0

    lax.fori_loop(0, NX, sum_b, 0)
    c_b2 = [send(mid_b.at[xs[o]], got_b2.at[o - 1], s_b2.at[o - 1], r_b2.at[o - 1], to_x[o]) for o in range(1, NX)]
    for cp in c_a2:
        cp.wait_recv()
    v = mid_a[y].astype(F32)
    for o in range(NY - 1):
        v = v + got_a2[o].astype(F32)
    zin[0:UA] = v.astype(BF)
    for cp in c_b2:
        cp.wait_recv()
    v = mid_b[x].astype(F32)
    for o in range(NX - 1):
        v = v + got_b2[o].astype(F32)
    zin[UA:UN] = v.astype(BF)
    zin[UN] = jnp.zeros((16, 128), BF)

    c_z = [send(zin.at[zs[o]], got_z.at[o - 1], s_z.at[o - 1], r_z.at[o - 1], to_z[o]) for o in range(1, NZ)]
    v = zin[z].astype(F32)
    for o in range(NZ - 1):
        c_z[o].wait_recv()
        v = v + got_z[o].astype(F32)
    fin[low, x, z] = v.astype(BF)
    own = fin.at[low, x, z]
    c_gz = [send(own, own, s_gz.at[o - 1], r_gz.at[o - 1], to_z[o]) for o in range(1, NZ)]
    for cp in c_gz:
        cp.wait_recv()
    own = fin.at[low, x]
    c_gx = [send(own, own, s_gx.at[o - 1], r_gx.at[o - 1], to_x[o]) for o in range(1, NX)]
    for cp in c_gx:
        cp.wait_recv()
    own = fin.at[low]
    c_gy = send(own, own, s_gy.at[0], r_gy.at[0], device(x, h * 2 + 1 - low, z, c))
    c_gy.wait_recv()
    for t in range(TILES):
        l, xo, u = t // (NX * UN), (t // UN) % NX, t % UN
        row, col = (t // 9) * 16, (t % 9) * 128
        g_proj[row : row + 16, col : col + 128] = fin[l, xo, u]
    for cp in pending:
        cp.wait_send()


def local(image_emb, text_feat, text_proj, pos_index, scale, bias):
    dma = lambda *shape: [pltpu.SemaphoreType.DMA(shape), pltpu.SemaphoreType.DMA(shape)]
    vm = pltpu.VMEM
    scratch = [
        vm((D, D), BF), vm((ROWS, D), BF), vm((ROWS, D), BF),
        vm((NH, 2, SH, ROWS), BF), vm((NH, SH, ROWS), BF),
        vm((ROWS, D), BF), vm((ROWS, D), BF), vm((ROWS, D), BF), vm((ROWS, D), BF),
        vm((ROWS, 1), F32), vm((ROWS, 1), F32), vm((ROWS, 1), F32),
        vm((ROWS, D), F32), vm((ROWS, D), F32), vm((ROWS, D), F32), vm((ROWS, D), F32),
        vm((ROWS, D), BF), vm((ROWS, D), BF), vm((NH, SH, D), F32),
        vm((NX, NY, UA, 16, 128), BF), vm((NY, NX, UB, 16, 128), BF),
        vm((NX - 1, NY, UA, 16, 128), BF), vm((NY - 1, NX, UB, 16, 128), BF),
        vm((NY, UA, 16, 128), BF), vm((NX, UB, 16, 128), BF),
        vm((NY - 1, UA, 16, 128), BF), vm((NX - 1, UB, 16, 128), BF),
        vm((NZ, 16, 128), BF), vm((NZ - 1, 16, 128), BF), vm((2, NX, NZ, 16, 128), BF),
    ]
    sems = (
        dma(IMG) + dma(1) + dma(3) + dma(3) + dma(3, NX - 1) + dma(4) + dma(1) + dma(1)
        + dma(NX - 1) + dma(NY - 1) + dma(NY - 1) + dma(NX - 1)
        + dma(NZ - 1) + dma(NZ - 1) + dma(NX - 1) + dma(1)
    )
    whole = pl.BlockSpec(memory_space=pltpu.VMEM)
    scalar = pl.BlockSpec(memory_space=pltpu.SMEM)
    g_image, g_feat, g_proj = pl.pallas_call(
        kernel,
        out_shape=(
            jax.ShapeDtypeStruct((ROWS, D), BF),
            jax.ShapeDtypeStruct((ROWS, D), BF),
            jax.ShapeDtypeStruct((SH, D), BF),
        ),
        in_specs=[whole, whole, whole, whole, scalar, scalar],
        out_specs=(whole, whole, whole),
        scratch_shapes=scratch + sems,
        compiler_params=pltpu.CompilerParams(
            collective_id=0, has_side_effects=True, vmem_limit_bytes=44 * 1024 * 1024
        ),
        name="contrast_back",
    )(image_emb, text_feat, text_proj, pos_index, scale, bias)
    return g_image.astype(F32), g_feat.astype(F32), g_proj.astype(F32)


def solution(mesh):
    return jax.shard_map(
        local,
        mesh=mesh,
        in_specs=(
            P(("blk", "dp"), None),
            P(("blk", "dp"), None),
            P("dp", None),
            P(("blk", "dp"), None),
            P(),
            P(),
        ),
        out_specs=(P(("blk", "dp"), None), P(("blk", "dp"), None), P("dp", None)),
        check_vma=False,
    )
```

```python
import jax
import jax.numpy as jnp
from jax import lax
from jax.experimental import pallas as pl
from jax.experimental.pallas import tpu as pltpu
from jax.sharding import PartitionSpec as P

MESH = pl.DeviceIdType.MESH
BF = jnp.bfloat16
F32 = jnp.float32
NX, NY, NZ, NH = 4, 8, 12, 4
ROWS, D, SH = 256, 1152, 144
PART = 32
UA, UB = 8, 3
UN = UA + UB
TILES = 81
COLS = 384
IMG = 4
VIA = 2


def place():
    b, d = lax.axis_index("blk"), lax.axis_index("dp")
    x = b // (2 * NZ)
    low = lax.rem(b // NZ, 2)
    z = lax.rem(b, NZ)
    return b, d, x, (d // 2) * 2 + low, z, lax.rem(d, 2)


def device(x, y, z, c):
    return (x * (2 * NZ) + lax.rem(y, 2) * NZ + z, (y // 2) * 2 + c)


def nt_dot(a, b):
    return lax.dot_general(a, b, (((1,), (1,)), ((), ())), preferred_element_type=F32)


def nn_dot(a, b):
    return jnp.dot(a, b, preferred_element_type=F32)


def sigmoid(v):
    return 1.0 / (1.0 + jnp.exp(-v))


def inv_norm(v):
    return lax.rsqrt(jnp.sum(v * v, axis=-1, keepdims=True) + 1e-06)


def unit_rows(src, unit, inv, step=64):
    def body(i, _):
        rows = pl.ds(pl.multiple_of(i * step, step), step)
        v = src[rows].astype(F32)
        r = inv_norm(v)
        unit[rows] = (v * r).astype(BF)
        if inv is not None:
            inv[rows] = r
        return 0

    lax.fori_loop(0, src.shape[0] // step, body, 0)


def norm_back(src, inv, grad, factor, out, step, done=None):
    for i in range(src.shape[0] // step):
        rows = pl.ds(i * step, step)
        v, r, g = src[rows].astype(F32), inv[rows], factor * grad[rows]
        inner = jnp.sum(v * g, axis=-1, keepdims=True)
        out[rows] = (r * (g - v * (inner * r * r))).astype(out.dtype)
        if done is not None:
            done(i, rows)


def by_columns(fn):
    def body(i, _):
        fn(pl.ds(pl.multiple_of(i * COLS, COLS), COLS))
        return 0

    lax.fori_loop(0, D // COLS, body, 0)


def kernel(
    image_h, feat_h, proj_h, pos_h, scale, bias,
    g_image, g_feat, g_proj,
    full, image, feat, pos, image_n, feat_p, feat_k, tft, tft_o, unit_in, unit_tp, inv_i, inv_t,
    text, text_p, acc_t, acc_i, coef_o, gte, gte_o, part, send_a, send_b, got_a, got_b,
    mid_a, mid_b, got_a2, got_b2, zin, got_z, fin,
    hop, s_in, relay, s_fwd, r_hop,
    s_img, r_img, s_txt, r_txt, s_py, r_py, s_pt, r_pt, s_px, r_px, s_pc, r_pc,
    s_tf, r_tf, s_ge, r_ge, s_a, r_a, s_b, r_b, s_a2, r_a2, s_b2, r_b2,
    s_z, r_z, s_gz, r_gz, s_gx, r_gx, s_gy, r_gy,
):
    b, d, x, y, z, c = place()
    n_blk = lax.axis_size("blk")
    h, low = y // 2, lax.rem(y, 2)
    prev = (lax.rem(b + n_blk - 1, n_blk), d)
    nxt = (lax.rem(b + 1, n_blk), d)
    mate = device(x, y, z, 1 - c)
    xs = [lax.rem(x + o, NX) for o in range(NX)]
    ys = [lax.rem(y + o, NY) for o in range(NY)]
    zs = [lax.rem(z + o, NZ) for o in range(NZ)]
    to_x = [device(v, y, z, c) for v in xs]
    to_y = [device(x, v, z, c) for v in ys]
    to_z = [device(x, y, v, c) for v in zs]
    pending = []
    col = x * 2 + low
    before, after = lax.rem(col + 7, 8), lax.rem(col + 1, 8)
    to_before = device(before // 2, 2 * h + lax.rem(before, 2), z, c)
    to_after = device(after // 2, 2 * h + lax.rem(after, 2), z, c)

    def copy(src, dst, s, r, dev):
        return pltpu.make_async_remote_copy(
            src_ref=src, dst_ref=dst, send_sem=s, recv_sem=r, device_id=dev, device_id_type=MESH
        )

    def send(src, dst, s, r, dev):
        cp = copy(src, dst, s, r, dev)
        cp.start()
        pending.append(cp)
        return cp

    def rows16(start, size):
        return pl.ds(pl.multiple_of(start, 16), size)

    barrier = pltpu.get_barrier_semaphore()
    partners = to_x[1:] + to_y[1:] + [mate, prev, nxt, to_z[1], to_z[NZ - 1], to_before, to_after]
    for dev in partners:
        pl.semaphore_signal(barrier, inc=1, device_id=dev, device_id_type=MESH)
    mine = d * SH
    loads = [
        pltpu.make_async_copy(a, to, s_in.at[i])
        for i, (a, to) in enumerate(
            ((image_h, image), (feat_h, feat), (proj_h, full.at[rows16(mine, SH)]), (pos_h, pos))
        )
    ]
    for cp in loads:
        cp.start()
    pl.semaphore_wait(barrier, len(partners))

    def pass_on(i):
        if i:
            pl.semaphore_wait(relay.at[i - 1], 2)
        if i < 5:
            for dev in (to_z[1], to_z[NZ - 1]):
                pl.semaphore_signal(relay.at[i], inc=1, device_id=dev, device_id_type=MESH)

    step = ROWS // IMG
    direct = IMG - VIA
    cut = lambda ref, i: ref.at[pl.ds(i * step, step)]
    c_img = [copy(cut(image_h, i), cut(image_n, i), s_img.at[i], r_img.at[i], prev) for i in range(IMG)]
    c_hop = [
        copy(cut(image_h, direct + i), cut(hop, i), s_img.at[direct + i], r_hop.at[i], to_before) for i in range(VIA)
    ]
    c_fwd = [
        copy(cut(hop, i), cut(image_n, direct + i), s_fwd.at[i], r_img.at[direct + i], to_z[NZ - 1])
        for i in range(VIA)
    ]
    c_txt = copy(feat_h, feat_p, s_txt.at[0], r_txt.at[0], nxt)
    pending += c_img + [c_txt]
    for i in range(direct):
        c_img[i].start()

    @pl.when(z == 0)
    def _():
        for i in range(VIA):
            c_hop[i].start()

    @pl.when(z != 0)
    def _():
        for i in range(VIA):
            c_img[direct + i].start()

    sign = 2 * low - 1
    xrow = x * PART
    rest = SH - NX * PART
    c_py, c_pt = [], []
    ahead = [device(x, lax.rem(y + sign * (k + 1) + NY, NY), z, c) for k in range(3)]
    for k in range(3):
        c_py.append(
            send(
                proj_h.at[rows16(xrow, PART)], full.at[rows16(mine + xrow, PART)],
                s_py.at[k], r_py.at[k], ahead[k],
            )
        )
    c_pc = [[], [], [], [send(proj_h, full.at[rows16(mine, SH)], s_pc.at[15], r_pc.at[15], mate)]]
    for k in range(3):
        c_pt.append(
            send(
                proj_h.at[pl.ds(NX * PART, rest)], full.at[rows16(mine + NX * PART, rest)],
                s_pt.at[k], r_pt.at[k], ahead[k],
            )
        )

    @pl.when(z != NZ - 1)
    def _():
        c_txt.start()

    for cp in loads:
        cp.wait()
    turned = feat[...].T
    for i in range(8):
        tft[i % 2, i // 2] = turned[i * SH : (i + 1) * SH]
    c_tf = send(tft.at[1 - c], tft_o, s_tf.at[0], r_tf.at[0], mate)
    unit_rows(image, unit_in.at[pl.ds(0, ROWS)], inv_i)
    for i in range(NH):
        feat_k[i] = feat[:, i * 2 * SH : (i + 1) * 2 * SH]

    pairs, rows_of = [], []
    for hop in (1, -2, 3):
        src_y = lax.rem(y + sign * hop + NY, NY)
        pairs.append(src_y // 2)
        rows_of.append(((src_y // 2) * 2 + c) * SH)

    def to_mate(k, i, start, size):
        where = full.at[rows16(start, size)]
        c_pc[k].append(send(where, where, s_pc.at[k * 5 + i], r_pc.at[k * 5 + i], mate))

    c_px = []
    for k in range(3):
        c_py[k].wait_recv()
        where = full.at[rows16(rows_of[k] + xrow, PART)]
        c_px.append([send(where, where, s_px.at[k, o - 1], r_px.at[k, o - 1], to_x[o]) for o in range(1, NX)])
        to_mate(k, 0, rows_of[k] + xrow, PART)

    @pl.when(z == 0)
    def _():
        for i in range(VIA):
            c_hop[i].wait_recv()
            c_fwd[i].start()

    def add_text(pair, first):
        rhs_rows = rows16(pair * (2 * SH), 2 * SH)

        def cols_of(cols):
            v = nn_dot(feat_k[pair], full[rhs_rows, cols])
            text[:, cols] = v if first else text[:, cols] + v

        by_columns(cols_of)

    c_pc[3][0].wait_recv()
    add_text(h, True)
    for k in range(3):
        for o in range(1, NX):
            c_px[k][o - 1].wait_recv()
            to_mate(k, o, rows_of[k] + lax.rem(x + NX - o, NX) * PART, PART)
        c_pt[k].wait_recv()
        to_mate(k, 4, rows_of[k] + NX * PART, rest)
        if k:
            for cp in c_pc[k - 1]:
                cp.wait_recv()
            add_text(pairs[k - 1], False)

    @pl.when(z == NZ - 1)
    def _():
        c_txt.start()

    for i in range(IMG):
        c_img[i].wait_recv()
        unit_rows(image_n.at[pl.ds(i * step, step)], unit_in.at[pl.ds(ROWS + i * step, step)], None)
    for cp in c_pc[2]:
        cp.wait_recv()
    add_text(pairs[2], False)
    unit_t = unit_tp.at[pl.ds(0, ROWS)]
    unit_rows(text, unit_t, inv_t)
    factor = scale[0]
    offset = bias[0]

    logit = factor * nt_dot(unit_t[...], unit_in[...]) + offset
    hit = lax.broadcasted_iota(jnp.int32, (ROWS, ROWS), 0) == pos[...]
    label = jnp.where(hit, 1.0, -1.0).astype(F32)
    coef = (-label * sigmoid(-label * logit[:, :ROWS])).astype(BF)
    coef_o[...] = coef
    coef_all = jnp.concatenate([coef, sigmoid(logit[:, ROWS:]).astype(BF)], axis=1)

    def text_grads(cols):
        acc_t[:, cols] = nn_dot(coef_all, unit_in[:, cols])

    by_columns(text_grads)
    c_ge = []

    def share(i, rows):
        c_ge.append(send(gte.at[rows], gte_o.at[rows], s_ge.at[i], r_ge.at[i], mate))

    norm_back(text, inv_t, acc_t, factor, gte, 64, share)
    pass_on(0)
    tft_c = tft[c].reshape(NH * SH, ROWS)

    def first_half(cols):
        part[:, cols] = nn_dot(tft_c, gte[:, cols])

    by_columns(first_half)
    pass_on(1)
    c_tf.wait_recv()
    for cp in c_ge:
        cp.wait_recv()

    def group(i):
        return lax.rem(h + 1 + i, NH)

    def second_half(i):
        hh = group(i)
        both = (part[rows16(hh * SH, SH)] + nn_dot(tft_o[hh], gte_o[...])).astype(BF)
        for t in range(2 * NX * UN):
            l, xo, u = t // (NX * UN), (t // UN) % NX, t % UN
            if t < TILES:
                row, col = (t // 9) * 16, (t % 9) * 128
                tile = both[row : row + 16, col : col + 128]
            else:
                tile = jnp.zeros((16, 128), BF)
            if u < UA:
                send_a[xo, 2 * hh + l, u] = tile
            else:
                send_b[2 * hh + l, xo, u - UA] = tile

    def a_copy(i, o):
        two = pl.ds(2 * group(i), 2)
        return copy(send_a.at[xs[o], two], got_a.at[o - 1, two], s_a.at[o - 1, i], r_a.at[o - 1, i], to_x[o])

    def b_copy(to):
        return copy(send_b.at[to], got_b.at[y], s_b.at[to], r_b.at[y], device(x, to, z, c))

    def a2_copy(to):
        return copy(mid_a.at[to], got_a2.at[y], s_a2.at[to], r_a2.at[y], device(x, to, z, c))

    def start_group(i, _):
        second_half(i)
        for o in range(1, NX):
            a_copy(i, o).start()
        for l in range(2):
            b_copy(2 * group(i) + l).start()
        return 0

    twin = 2 * h + 1 - low
    lax.fori_loop(0, NH - 1, start_group, 0)
    second_half(NH - 1)
    for o in range(1, NX):
        a_copy(NH - 1, o).start()
    b_copy(twin).start()
    pass_on(2)

    def feat_cols(i, _):
        cols = pl.ds(pl.multiple_of(i * COLS, COLS), COLS)
        g_feat[:, cols] = nt_dot(gte[...], full[cols]).astype(BF)
        return 0

    lax.fori_loop(0, D // COLS, feat_cols, 0)

    def sum_a(i):
        for o in range(1, NX):
            a_copy(i, o).wait_recv()
        for l in range(2):
            at = 2 * group(i) + l
            v = send_a[x, at].astype(F32)
            for o in range(NX - 1):
                v = v + got_a[o, at].astype(F32)
            mid_a[at] = v.astype(BF)

    def a_group(i, _):
        sum_a(i)
        for l in range(2):
            a2_copy(2 * group(i) + l).start()
        return 0

    pass_on(3)
    lax.fori_loop(0, NH - 1, a_group, 0)
    sum_a(NH - 1)
    a2_copy(twin).start()
    pass_on(4)

    def received(sem, slots, at):
        copy(slots.at[at], slots.at[at], sem.at[at], sem.at[at], mate).wait_recv()

    for o in range(1, NY):
        received(r_b, got_b, ys[o])

    def sum_b(i, _):
        v = send_b[y, i].astype(F32)
        for o in range(1, NY):
            v = v + got_b[ys[o], i].astype(F32)
        mid_b[i] = v.astype(BF)
        return 0

    lax.fori_loop(0, NX, sum_b, 0)
    c_b2 = [send(mid_b.at[xs[o]], got_b2.at[o - 1], s_b2.at[o - 1], r_b2.at[o - 1], to_x[o]) for o in range(1, NX)]

    for o in range(1, NY):
        received(r_a2, got_a2, ys[o])
    v = mid_a[y].astype(F32)
    for o in range(1, NY):
        v = v + got_a2[ys[o]].astype(F32)
    zin[0:UA] = v.astype(BF)
    for cp in c_b2:
        cp.wait_recv()
    v = mid_b[x].astype(F32)
    for o in range(NX - 1):
        v = v + got_b2[o].astype(F32)
    zin[UA:UN] = v.astype(BF)
    zin[UN] = jnp.zeros((16, 128), BF)

    pass_on(5)
    c_z = [send(zin.at[zs[o]], got_z.at[o - 1], s_z.at[o - 1], r_z.at[o - 1], to_z[o]) for o in range(1, NZ)]
    v = zin[z].astype(F32)
    for o in range(NZ - 1):
        c_z[o].wait_recv()
        v = v + got_z[o].astype(F32)
    fin[low, x, z] = v.astype(BF)
    own = fin.at[low, x, z]
    c_gz = [send(own, own, s_gz.at[o - 1], r_gz.at[o - 1], to_z[o]) for o in range(1, NZ)]

    c_txt.wait_recv()

    def text_p_cols(cols):
        text_p[:, cols] = nn_dot(feat_p[...], full[:, cols])

    by_columns(text_p_cols)
    unit_rows(text_p, unit_tp.at[pl.ds(ROWS, ROWS)], None)
    near_p = sigmoid(factor * nt_dot(unit_in[:ROWS], unit_tp[ROWS:]) + offset).astype(BF)
    coef_both = jnp.concatenate([coef_o[...].T, near_p], axis=1)

    def image_cols(cols):
        acc_i[:, cols] = nn_dot(coef_both, unit_tp[:, cols])

    by_columns(image_cols)
    norm_back(image, inv_i, acc_i, factor, g_image, 64)

    for cp in c_gz:
        cp.wait_recv()
    own = fin.at[low, x, pl.ds(0, UN)]
    c_gy = [send(own, own, s_gy.at[0], r_gy.at[0], device(x, twin, z, c))]
    c_gx = [send(own, own, s_gx.at[o - 1], r_gx.at[o - 1], to_x[o]) for o in range(1, NX)]
    for o in (1, 3, 2):
        c_gx[o - 1].wait_recv()
        got = fin.at[low, xs[NX - o], pl.ds(0, UN)]
        c_gy.append(send(got, got, s_gy.at[o], r_gy.at[o], device(x, twin, z, c)))
    for cp in c_gy:
        cp.wait_recv()
    for t in range(TILES):
        l, xo, u = t // (NX * UN), (t // UN) % NX, t % UN
        row, col = (t // 9) * 16, (t % 9) * 128
        g_proj[row : row + 16, col : col + 128] = fin[l, xo, u]
    for cp in pending:
        cp.wait_send()
    for i in range(NH):
        for o in range(1, NX):
            a_copy(i, o).wait_send()
    for o in range(1, NY):
        b_copy(ys[o]).wait_send()
        a2_copy(ys[o]).wait_send()

    @pl.when(z == 0)
    def _():
        for cp in c_fwd:
            cp.wait_send()


def local(image_emb, text_feat, text_proj, pos_index, scale, bias):
    dma = lambda *shape: [pltpu.SemaphoreType.DMA(shape), pltpu.SemaphoreType.DMA(shape)]
    vm = pltpu.VMEM
    scratch = [
        vm((D, D), BF), vm((ROWS, D), BF), vm((ROWS, D), BF), vm((1, ROWS), jnp.int32),
        vm((ROWS, D), BF), vm((ROWS, D), BF), vm((NH, ROWS, 2 * SH), BF),
        vm((2, NH, SH, ROWS), BF), vm((NH, SH, ROWS), BF),
        vm((2 * ROWS, D), BF), vm((2 * ROWS, D), BF),
        vm((ROWS, 1), F32), vm((ROWS, 1), F32),
        vm((ROWS, D), F32), vm((ROWS, D), F32), vm((ROWS, D), F32), vm((ROWS, D), F32),
        vm((ROWS, ROWS), BF), vm((ROWS, D), BF), vm((ROWS, D), BF), vm((NH * SH, D), F32),
        vm((NX, NY, UA, 16, 128), BF), vm((NY, NX, UB, 16, 128), BF),
        vm((NX - 1, NY, UA, 16, 128), BF), vm((NY, NX, UB, 16, 128), BF),
        vm((NY, UA, 16, 128), BF), vm((NX, UB, 16, 128), BF),
        vm((NY, UA, 16, 128), BF), vm((NX - 1, UB, 16, 128), BF),
        vm((NZ, 16, 128), BF), vm((NZ - 1, 16, 128), BF), vm((2, NX, NZ, 16, 128), BF),
        vm((VIA * ROWS // IMG, D), BF), pltpu.SemaphoreType.DMA((4,)), pltpu.SemaphoreType.REGULAR((5,)),
        pltpu.SemaphoreType.DMA((VIA,)), pltpu.SemaphoreType.DMA((VIA,)),
    ]
    sems = (
        dma(IMG) + dma(1) + dma(3) + dma(3) + dma(3, NX - 1) + dma(16) + dma(1) + dma(4)
        + dma(NX - 1, NH) + dma(NY) + dma(NY) + dma(NX - 1)
        + dma(NZ - 1) + dma(NZ - 1) + dma(NX - 1) + dma(NX)
    )
    whole = pl.BlockSpec(memory_space=pltpu.VMEM)
    scalar = pl.BlockSpec(memory_space=pltpu.SMEM)
    far = pl.BlockSpec(memory_space=pltpu.HBM)
    g_image, g_feat, g_proj = pl.pallas_call(
        kernel,
        out_shape=(
            jax.ShapeDtypeStruct((ROWS, D), BF),
            jax.ShapeDtypeStruct((ROWS, D), BF),
            jax.ShapeDtypeStruct((SH, D), BF),
        ),
        in_specs=[far, far, far, far, scalar, scalar],
        out_specs=(whole, whole, whole),
        scratch_shapes=scratch + sems,
        compiler_params=pltpu.CompilerParams(
            collective_id=0, has_side_effects=True, vmem_limit_bytes=58 * 1024 * 1024
        ),
        name="contrast_back",
    )(image_emb, text_feat, text_proj, pos_index, scale, bias)
    return g_image.astype(F32), g_feat.astype(F32), g_proj.astype(F32)


def solution(mesh):
    return jax.shard_map(
        local,
        mesh=mesh,
        in_specs=(
            P(("blk", "dp"), None),
            P(("blk", "dp"), None),
            P("dp", None),
            P(("blk", "dp"), None),
            P(),
            P(),
        ),
        out_specs=(P(("blk", "dp"), None), P(("blk", "dp"), None), P("dp", None)),
        check_vma=False,
    )
```

```python
import jax
import jax.numpy as jnp
from jax import lax
from jax.experimental import pallas as pl
from jax.experimental.pallas import tpu as pltpu
from jax.sharding import PartitionSpec as P

MESH = pl.DeviceIdType.MESH
BF = jnp.bfloat16
F32 = jnp.float32
NX, NY, NZ, NH = 4, 8, 12, 4
ROWS, D, SH = 256, 1152, 144
PART = 32
UA, UB = 8, 3
UN = UA + UB
TILES = 81
COLS = 384
IMG = 4
VIA = 2


def place():
    b, d = lax.axis_index("blk"), lax.axis_index("dp")
    x = b // (2 * NZ)
    low = lax.rem(b // NZ, 2)
    z = lax.rem(b, NZ)
    return b, d, x, (d // 2) * 2 + low, z, lax.rem(d, 2)


def device(x, y, z, c):
    return (x * (2 * NZ) + lax.rem(y, 2) * NZ + z, (y // 2) * 2 + c)


def nt_dot(a, b):
    return lax.dot_general(a, b, (((1,), (1,)), ((), ())), preferred_element_type=F32)


def nn_dot(a, b):
    return jnp.dot(a, b, preferred_element_type=F32)


def sigmoid(v):
    return 1.0 / (1.0 + jnp.exp(-v))


def inv_norm(v):
    return lax.rsqrt(jnp.sum(v * v, axis=-1, keepdims=True) + 1e-06)


def unit_rows(src, unit, inv, step=64):
    def body(i, _):
        rows = pl.ds(pl.multiple_of(i * step, step), step)
        v = src[rows].astype(F32)
        r = inv_norm(v)
        unit[rows] = (v * r).astype(BF)
        if inv is not None:
            inv[rows] = r
        return 0

    lax.fori_loop(0, src.shape[0] // step, body, 0)


def norm_back(src, inv, grad, factor, out, step, done=None):
    for i in range(src.shape[0] // step):
        rows = pl.ds(i * step, step)
        v, r, g = src[rows].astype(F32), inv[rows], factor * grad[rows]
        inner = jnp.sum(v * g, axis=-1, keepdims=True)
        out[rows] = (r * (g - v * (inner * r * r))).astype(out.dtype)
        if done is not None:
            done(i, rows)


def by_columns(fn):
    def body(i, _):
        fn(pl.ds(pl.multiple_of(i * COLS, COLS), COLS))
        return 0

    lax.fori_loop(0, D // COLS, body, 0)


def kernel(
    image_h, feat_h, proj_h, pos_h, scale, bias,
    g_image, g_feat, g_proj,
    full, image, feat, pos, image_n, feat_p, feat_k, tft, tft_o, unit_in, unit_tp, inv_i, inv_t,
    text, text_p, acc_t, acc_i, coef_o, gte, gte_o, part, send_a, send_b, got_a, got_b,
    mid_a, mid_b, got_a2, got_b2, zin, got_z, fin,
    hop, hop_t, f_image, f_feat, f_proj, s_in, s_out, relay, s_fwd, r_hop,
    s_img, r_img, s_txt, r_txt, s_py, r_py, s_pt, r_pt, s_px, r_px, s_pc, r_pc,
    s_tf, r_tf, s_ge, r_ge, s_a, r_a, s_b, r_b, s_a2, r_a2, s_b2, r_b2,
    s_z, r_z, s_gz, r_gz, s_gx, r_gx, s_gy, r_gy,
):
    b, d, x, y, z, c = place()
    n_blk = lax.axis_size("blk")
    h, low = y // 2, lax.rem(y, 2)
    prev = (lax.rem(b + n_blk - 1, n_blk), d)
    nxt = (lax.rem(b + 1, n_blk), d)
    mate = device(x, y, z, 1 - c)
    xs = [lax.rem(x + o, NX) for o in range(NX)]
    ys = [lax.rem(y + o, NY) for o in range(NY)]
    zs = [lax.rem(z + o, NZ) for o in range(NZ)]
    to_x = [device(v, y, z, c) for v in xs]
    to_y = [device(x, v, z, c) for v in ys]
    to_z = [device(x, y, v, c) for v in zs]
    pending = []
    col = x * 2 + low
    before, after = lax.rem(col + 7, 8), lax.rem(col + 1, 8)
    to_before = device(before // 2, 2 * h + lax.rem(before, 2), z, c)
    to_after = device(after // 2, 2 * h + lax.rem(after, 2), z, c)

    def copy(src, dst, s, r, dev):
        return pltpu.make_async_remote_copy(
            src_ref=src, dst_ref=dst, send_sem=s, recv_sem=r, device_id=dev, device_id_type=MESH
        )

    def send(src, dst, s, r, dev):
        cp = copy(src, dst, s, r, dev)
        cp.start()
        pending.append(cp)
        return cp

    def rows16(start, size):
        return pl.ds(pl.multiple_of(start, 16), size)

    barrier = pltpu.get_barrier_semaphore()
    partners = to_x[1:] + to_y[1:] + [mate, prev, nxt, to_z[1], to_z[NZ - 1], to_before, to_after]
    for dev in partners:
        pl.semaphore_signal(barrier, inc=1, device_id=dev, device_id_type=MESH)
    mine = d * SH
    loads = [
        pltpu.make_async_copy(a, to, s_in.at[i])
        for i, (a, to) in enumerate(
            ((image_h, image), (feat_h, feat), (proj_h, full.at[rows16(mine, SH)]), (pos_h, pos))
        )
    ]
    for cp in loads:
        cp.start()
    pl.semaphore_wait(barrier, len(partners))

    def pass_on(i):
        if i:
            pl.semaphore_wait(relay.at[i - 1], 2)
        if i < 5:
            for dev in (to_z[1], to_z[NZ - 1]):
                pl.semaphore_signal(relay.at[i], inc=1, device_id=dev, device_id_type=MESH)

    step = ROWS // IMG
    direct = IMG - VIA
    cut = lambda ref, i: ref.at[pl.ds(i * step, step)]
    c_img = [copy(cut(image_h, i), cut(image_n, i), s_img.at[i], r_img.at[i], prev) for i in range(IMG)]
    c_hop = [
        copy(cut(image_h, direct + i), cut(hop, i), s_img.at[direct + i], r_hop.at[i], to_before) for i in range(VIA)
    ]
    c_fwd = [
        copy(cut(hop, i), cut(image_n, direct + i), s_fwd.at[i], r_img.at[direct + i], to_z[NZ - 1])
        for i in range(VIA)
    ]
    half = lambda ref, i: ref.at[pl.ds(i * (ROWS // 2), ROWS // 2)]
    c_txt = [copy(half(feat_h, i), half(feat_p, i), s_txt.at[i], r_txt.at[i], nxt) for i in range(2)]
    t_hop = copy(half(feat_h, 1), hop_t, s_txt.at[1], r_hop.at[VIA], to_after)
    t_fwd = copy(hop_t, half(feat_p, 1), s_fwd.at[VIA], r_txt.at[1], to_z[1])
    pending += c_img + c_txt
    for i in range(direct):
        c_img[i].start()

    @pl.when(z == 0)
    def _():
        for i in range(VIA):
            c_hop[i].start()

    @pl.when(z != 0)
    def _():
        for i in range(VIA):
            c_img[direct + i].start()

    sign = 2 * low - 1
    xrow = x * PART
    rest = SH - NX * PART
    c_py, c_pt = [], []
    ahead = [device(x, lax.rem(y + sign * (k + 1) + NY, NY), z, c) for k in range(3)]
    for k in range(3):
        c_py.append(
            send(
                proj_h.at[rows16(xrow, PART)], full.at[rows16(mine + xrow, PART)],
                s_py.at[k], r_py.at[k], ahead[k],
            )
        )
    c_pc = [[], [], [], [send(proj_h, full.at[rows16(mine, SH)], s_pc.at[15], r_pc.at[15], mate)]]
    for k in range(3):
        c_pt.append(
            send(
                proj_h.at[pl.ds(NX * PART, rest)], full.at[rows16(mine + NX * PART, rest)],
                s_pt.at[k], r_pt.at[k], ahead[k],
            )
        )

    @pl.when(z != NZ - 1)
    def _():
        for cp in c_txt:
            cp.start()

    for cp in loads:
        cp.wait()
    turned = feat[...].T
    for i in range(8):
        tft[i % 2, i // 2] = turned[i * SH : (i + 1) * SH]
    c_tf = send(tft.at[1 - c], tft_o, s_tf.at[0], r_tf.at[0], mate)
    unit_rows(image, unit_in.at[pl.ds(0, ROWS)], inv_i)
    for i in range(NH):
        feat_k[i] = feat[:, i * 2 * SH : (i + 1) * 2 * SH]

    pairs, rows_of = [], []
    for hop in (1, -2, 3):
        src_y = lax.rem(y + sign * hop + NY, NY)
        pairs.append(src_y // 2)
        rows_of.append(((src_y // 2) * 2 + c) * SH)

    def to_mate(k, i, start, size):
        where = full.at[rows16(start, size)]
        c_pc[k].append(send(where, where, s_pc.at[k * 5 + i], r_pc.at[k * 5 + i], mate))

    c_px = []
    for k in range(3):
        c_py[k].wait_recv()
        where = full.at[rows16(rows_of[k] + xrow, PART)]
        c_px.append([send(where, where, s_px.at[k, o - 1], r_px.at[k, o - 1], to_x[o]) for o in range(1, NX)])
        to_mate(k, 0, rows_of[k] + xrow, PART)

    @pl.when(z == 0)
    def _():
        for i in range(VIA):
            c_hop[i].wait_recv()
            c_fwd[i].start()

    def add_text(pair, first):
        rhs_rows = rows16(pair * (2 * SH), 2 * SH)

        def cols_of(cols):
            v = nn_dot(feat_k[pair], full[rhs_rows, cols])
            text[:, cols] = v if first else text[:, cols] + v

        by_columns(cols_of)

    c_pc[3][0].wait_recv()
    add_text(h, True)
    for k in range(3):
        for o in range(1, NX):
            c_px[k][o - 1].wait_recv()
            to_mate(k, o, rows_of[k] + lax.rem(x + NX - o, NX) * PART, PART)
        c_pt[k].wait_recv()
        to_mate(k, 4, rows_of[k] + NX * PART, rest)
        if k:
            for cp in c_pc[k - 1]:
                cp.wait_recv()
            add_text(pairs[k - 1], False)

    @pl.when(z == NZ - 1)
    def _():
        c_txt[0].start()
        t_hop.start()

    for i in range(IMG):
        c_img[i].wait_recv()
        unit_rows(image_n.at[pl.ds(i * step, step)], unit_in.at[pl.ds(ROWS + i * step, step)], None)
    for cp in c_pc[2]:
        cp.wait_recv()
    add_text(pairs[2], False)
    unit_t = unit_tp.at[pl.ds(0, ROWS)]
    unit_rows(text, unit_t, inv_t)
    factor = scale[0]
    offset = bias[0]

    logit = factor * nt_dot(unit_t[...], unit_in[...]) + offset
    hit = lax.broadcasted_iota(jnp.int32, (ROWS, ROWS), 0) == pos[...]
    label = jnp.where(hit, 1.0, -1.0).astype(F32)
    coef = (-label * sigmoid(-label * logit[:, :ROWS])).astype(BF)
    coef_o[...] = coef
    coef_all = jnp.concatenate([coef, sigmoid(logit[:, ROWS:]).astype(BF)], axis=1)

    def text_grads(cols):
        acc_t[:, cols] = nn_dot(coef_all, unit_in[:, cols])

    by_columns(text_grads)
    c_ge = []

    def share(i, rows):
        c_ge.append(send(gte.at[rows], gte_o.at[rows], s_ge.at[i], r_ge.at[i], mate))

    norm_back(text, inv_t, acc_t, factor, gte, 64, share)
    pass_on(0)
    tft_c = tft[c].reshape(NH * SH, ROWS)

    def first_half(cols):
        part[:, cols] = nn_dot(tft_c, gte[:, cols])

    by_columns(first_half)
    pass_on(1)
    c_tf.wait_recv()
    for cp in c_ge:
        cp.wait_recv()

    def group(i):
        return lax.rem(h + 1 + i, NH)

    def second_half(i):
        hh = group(i)
        both = (part[rows16(hh * SH, SH)] + nn_dot(tft_o[hh], gte_o[...])).astype(BF)
        for t in range(2 * NX * UN):
            l, xo, u = t // (NX * UN), (t // UN) % NX, t % UN
            if t < TILES:
                row, col = (t // 9) * 16, (t % 9) * 128
                tile = both[row : row + 16, col : col + 128]
            else:
                tile = jnp.zeros((16, 128), BF)
            if u < UA:
                send_a[xo, 2 * hh + l, u] = tile
            else:
                send_b[2 * hh + l, xo, u - UA] = tile

    def a_copy(i, o):
        two = pl.ds(2 * group(i), 2)
        return copy(send_a.at[xs[o], two], got_a.at[o - 1, two], s_a.at[o - 1, i], r_a.at[o - 1, i], to_x[o])

    def b_copy(to):
        return copy(send_b.at[to], got_b.at[y], s_b.at[to], r_b.at[y], device(x, to, z, c))

    def a2_copy(to):
        return copy(mid_a.at[to], got_a2.at[y], s_a2.at[to], r_a2.at[y], device(x, to, z, c))

    def start_group(i, _):
        second_half(i)
        for o in range(1, NX):
            a_copy(i, o).start()
        for l in range(2):
            b_copy(2 * group(i) + l).start()
        return 0

    twin = 2 * h + 1 - low
    lax.fori_loop(0, NH - 1, start_group, 0)
    second_half(NH - 1)
    for o in range(1, NX):
        a_copy(NH - 1, o).start()
    b_copy(twin).start()
    pass_on(2)

    @pl.when(z == NZ - 1)
    def _():
        t_hop.wait_recv()
        t_fwd.start()

    def feat_cols(i, _):
        cols = pl.ds(pl.multiple_of(i * COLS, COLS), COLS)
        f_feat[:, cols] = nt_dot(gte[...], full[cols]).astype(BF)
        return 0

    lax.fori_loop(0, D // COLS, feat_cols, 0)
    out_feat = pltpu.make_async_copy(f_feat, g_feat, s_out.at[0])
    out_feat.start()

    def sum_a(i):
        for o in range(1, NX):
            a_copy(i, o).wait_recv()
        for l in range(2):
            at = 2 * group(i) + l
            v = send_a[x, at].astype(F32)
            for o in range(NX - 1):
                v = v + got_a[o, at].astype(F32)
            mid_a[at] = v.astype(BF)

    def a_group(i, _):
        sum_a(i)
        for l in range(2):
            a2_copy(2 * group(i) + l).start()
        return 0

    pass_on(3)
    lax.fori_loop(0, NH - 1, a_group, 0)
    sum_a(NH - 1)
    a2_copy(twin).start()
    pass_on(4)

    def received(sem, slots, at):
        copy(slots.at[at], slots.at[at], sem.at[at], sem.at[at], mate).wait_recv()

    for o in range(1, NY):
        received(r_b, got_b, ys[o])

    def sum_b(i, _):
        v = send_b[y, i].astype(F32)
        for o in range(1, NY):
            v = v + got_b[ys[o], i].astype(F32)
        mid_b[i] = v.astype(BF)
        return 0

    lax.fori_loop(0, NX, sum_b, 0)
    c_b2 = [send(mid_b.at[xs[o]], got_b2.at[o - 1], s_b2.at[o - 1], r_b2.at[o - 1], to_x[o]) for o in range(1, NX)]

    for o in range(1, NY):
        received(r_a2, got_a2, ys[o])
    v = mid_a[y].astype(F32)
    for o in range(1, NY):
        v = v + got_a2[ys[o]].astype(F32)
    zin[0:UA] = v.astype(BF)
    for cp in c_b2:
        cp.wait_recv()
    v = mid_b[x].astype(F32)
    for o in range(NX - 1):
        v = v + got_b2[o].astype(F32)
    zin[UA:UN] = v.astype(BF)
    zin[UN] = jnp.zeros((16, 128), BF)

    pass_on(5)
    c_z = [send(zin.at[zs[o]], got_z.at[o - 1], s_z.at[o - 1], r_z.at[o - 1], to_z[o]) for o in range(1, NZ)]
    v = zin[z].astype(F32)
    for o in range(NZ - 1):
        c_z[o].wait_recv()
        v = v + got_z[o].astype(F32)
    fin[low, x, z] = v.astype(BF)
    own = fin.at[low, x, z]
    c_gz = [send(own, own, s_gz.at[o - 1], r_gz.at[o - 1], to_z[o]) for o in range(1, NZ)]

    for cp in c_txt:
        cp.wait_recv()

    def text_p_cols(cols):
        text_p[:, cols] = nn_dot(feat_p[...], full[:, cols])

    by_columns(text_p_cols)
    unit_rows(text_p, unit_tp.at[pl.ds(ROWS, ROWS)], None)
    near_p = sigmoid(factor * nt_dot(unit_in[:ROWS], unit_tp[ROWS:]) + offset).astype(BF)
    coef_both = jnp.concatenate([coef_o[...].T, near_p], axis=1)

    def image_cols(cols):
        acc_i[:, cols] = nn_dot(coef_both, unit_tp[:, cols])

    by_columns(image_cols)
    norm_back(image, inv_i, acc_i, factor, f_image, 64)
    out_image = pltpu.make_async_copy(f_image, g_image, s_out.at[1])
    out_image.start()

    for cp in c_gz:
        cp.wait_recv()
    own = fin.at[low, x, pl.ds(0, UN)]
    c_gy = [send(own, own, s_gy.at[0], r_gy.at[0], device(x, twin, z, c))]
    c_gx = [send(own, own, s_gx.at[o - 1], r_gx.at[o - 1], to_x[o]) for o in range(1, NX)]
    for o in (1, 3, 2):
        c_gx[o - 1].wait_recv()
        got = fin.at[low, xs[NX - o], pl.ds(0, UN)]
        c_gy.append(send(got, got, s_gy.at[o], r_gy.at[o], device(x, twin, z, c)))
    for cp in c_gy:
        cp.wait_recv()
    for t in range(TILES):
        l, xo, u = t // (NX * UN), (t // UN) % NX, t % UN
        row, col = (t // 9) * 16, (t % 9) * 128
        f_proj[row : row + 16, col : col + 128] = fin[l, xo, u]
    out_proj = pltpu.make_async_copy(f_proj, g_proj, s_out.at[2])
    out_proj.start()
    for cp in pending:
        cp.wait_send()
    for i in range(NH):
        for o in range(1, NX):
            a_copy(i, o).wait_send()
    for o in range(1, NY):
        b_copy(ys[o]).wait_send()
        a2_copy(ys[o]).wait_send()

    @pl.when(z == 0)
    def _():
        for cp in c_fwd:
            cp.wait_send()

    @pl.when(z == NZ - 1)
    def _():
        t_fwd.wait_send()

    for cp in (out_feat, out_image, out_proj):
        cp.wait()


def widen(*refs):
    srcs, dsts, narrow, wide, (s_in, s_out) = refs[:3], refs[3:6], refs[6:9], refs[9:12], refs[12:]
    pieces = [(a, r, 64) for a in range(2) for r in range(0, ROWS, 64)] + [(2, r, 48) for r in range(0, SH, 48)]
    ins, outs = [], []
    for i, (a, r, n) in enumerate(pieces):
        rows = pl.ds(r, n)
        ins.append(pltpu.make_async_copy(srcs[a].at[rows], narrow[a].at[rows], s_in.at[i]))
        outs.append(pltpu.make_async_copy(wide[a].at[rows], dsts[a].at[rows], s_out.at[i]))
        ins[-1].start()
    for i, (a, r, n) in enumerate(pieces):
        ins[i].wait()
        wide[a][r : r + n] = narrow[a][r : r + n].astype(F32)
        outs[i].start()
    for cp in outs:
        cp.wait()


def local(image_emb, text_feat, text_proj, pos_index, scale, bias):
    dma = lambda *shape: [pltpu.SemaphoreType.DMA(shape), pltpu.SemaphoreType.DMA(shape)]
    vm = pltpu.VMEM
    scratch = [
        vm((D, D), BF), vm((ROWS, D), BF), vm((ROWS, D), BF), vm((1, ROWS), jnp.int32),
        vm((ROWS, D), BF), vm((ROWS, D), BF), vm((NH, ROWS, 2 * SH), BF),
        vm((2, NH, SH, ROWS), BF), vm((NH, SH, ROWS), BF),
        vm((2 * ROWS, D), BF), vm((2 * ROWS, D), BF),
        vm((ROWS, 1), F32), vm((ROWS, 1), F32),
        vm((ROWS, D), F32), vm((ROWS, D), F32), vm((ROWS, D), F32), vm((ROWS, D), F32),
        vm((ROWS, ROWS), BF), vm((ROWS, D), BF), vm((ROWS, D), BF), vm((NH * SH, D), F32),
        vm((NX, NY, UA, 16, 128), BF), vm((NY, NX, UB, 16, 128), BF),
        vm((NX - 1, NY, UA, 16, 128), BF), vm((NY, NX, UB, 16, 128), BF),
        vm((NY, UA, 16, 128), BF), vm((NX, UB, 16, 128), BF),
        vm((NY, UA, 16, 128), BF), vm((NX - 1, UB, 16, 128), BF),
        vm((NZ, 16, 128), BF), vm((NZ - 1, 16, 128), BF), vm((2, NX, NZ, 16, 128), BF),
        vm((VIA * ROWS // IMG, D), BF), vm((ROWS // 2, D), BF),
        vm((ROWS, D), BF), vm((ROWS, D), BF), vm((SH, D), BF),
        pltpu.SemaphoreType.DMA((4,)), pltpu.SemaphoreType.DMA((3,)), pltpu.SemaphoreType.REGULAR((5,)),
        pltpu.SemaphoreType.DMA((VIA + 1,)), pltpu.SemaphoreType.DMA((VIA + 1,)),
    ]
    sems = (
        dma(IMG) + dma(2) + dma(3) + dma(3) + dma(3, NX - 1) + dma(16) + dma(1) + dma(4)
        + dma(NX - 1, NH) + dma(NY) + dma(NY) + dma(NX - 1)
        + dma(NZ - 1) + dma(NZ - 1) + dma(NX - 1) + dma(NX)
    )
    scalar = pl.BlockSpec(memory_space=pltpu.SMEM)
    far = pl.BlockSpec(memory_space=pltpu.HBM)
    g_image, g_feat, g_proj = pl.pallas_call(
        kernel,
        out_shape=(
            jax.ShapeDtypeStruct((ROWS, D), BF),
            jax.ShapeDtypeStruct((ROWS, D), BF),
            jax.ShapeDtypeStruct((SH, D), BF),
        ),
        in_specs=[far, far, far, far, scalar, scalar],
        out_specs=(far, far, far),
        scratch_shapes=scratch + sems,
        compiler_params=pltpu.CompilerParams(
            collective_id=0, has_side_effects=True, vmem_limit_bytes=58 * 1024 * 1024
        ),
        name="contrast_back",
    )(image_emb, text_feat, text_proj, pos_index, scale, bias)
    sizes = ((ROWS, D), (ROWS, D), (SH, D))
    return pl.pallas_call(
        widen,
        out_shape=tuple(jax.ShapeDtypeStruct(n, F32) for n in sizes),
        in_specs=[far] * 3,
        out_specs=(far,) * 3,
        scratch_shapes=[vm(n, BF) for n in sizes] + [vm(n, F32) for n in sizes]
        + [pltpu.SemaphoreType.DMA((11,)), pltpu.SemaphoreType.DMA((11,))],
        compiler_params=pltpu.CompilerParams(vmem_limit_bytes=58 * 1024 * 1024),
        name="widen",
    )(g_image, g_feat, g_proj)


def solution(mesh):
    return jax.shard_map(
        local,
        mesh=mesh,
        in_specs=(
            P(("blk", "dp"), None),
            P(("blk", "dp"), None),
            P("dp", None),
            P(("blk", "dp"), None),
            P(),
            P(),
        ),
        out_specs=(P(("blk", "dp"), None), P(("blk", "dp"), None), P("dp", None)),
        check_vma=False,
    )
```

```python
import jax
import jax.numpy as jnp
from jax import lax
from jax.experimental import pallas as pl
from jax.experimental.pallas import tpu as pltpu
from jax.sharding import PartitionSpec as P

MESH = pl.DeviceIdType.MESH
BF = jnp.bfloat16
F32 = jnp.float32
NX, NY, NZ, NH = 4, 8, 12, 4
ROWS, D, SH = 256, 1152, 144
PART = 32
UA, UB = 8, 3
UN = UA + UB
TILES = 81
COLS = 384
IMG = 4


def place():
    b, d = lax.axis_index("blk"), lax.axis_index("dp")
    x = b // (2 * NZ)
    low = lax.rem(b // NZ, 2)
    z = lax.rem(b, NZ)
    return b, d, x, (d // 2) * 2 + low, z, lax.rem(d, 2)


def device(x, y, z, c):
    return (x * (2 * NZ) + lax.rem(y, 2) * NZ + z, (y // 2) * 2 + c)


def nt_dot(a, b):
    return lax.dot_general(a, b, (((1,), (1,)), ((), ())), preferred_element_type=F32)


def nn_dot(a, b):
    return jnp.dot(a, b, preferred_element_type=F32)


def sigmoid(v):
    return 1.0 / (1.0 + jnp.exp(-v))


def inv_norm(v):
    return lax.rsqrt(jnp.sum(v * v, axis=-1, keepdims=True) + 1e-06)


def unit_rows(src, unit, inv, step=64):
    def body(i, _):
        rows = pl.ds(pl.multiple_of(i * step, step), step)
        v = src[rows].astype(F32)
        r = inv_norm(v)
        unit[rows] = (v * r).astype(BF)
        if inv is not None:
            inv[rows] = r
        return 0

    lax.fori_loop(0, src.shape[0] // step, body, 0)


def norm_back(src, inv, grad, factor, out, step, done=None):
    for i in range(src.shape[0] // step):
        rows = pl.ds(i * step, step)
        v, r, g = src[rows].astype(F32), inv[rows], factor * grad[rows]
        inner = jnp.sum(v * g, axis=-1, keepdims=True)
        out[rows] = (r * (g - v * (inner * r * r))).astype(out.dtype)
        if done is not None:
            done(i, rows)


def by_columns(fn):
    def body(i, _):
        fn(pl.ds(pl.multiple_of(i * COLS, COLS), COLS))
        return 0

    lax.fori_loop(0, D // COLS, body, 0)


def kernel(
    image_h, feat_h, proj_h, pos_h, scale, bias,
    g_image, g_feat, g_proj,
    full, image, feat, pos, image_n, feat_p, feat_k, tft, tft_o, unit_in, unit_tp, inv_i, inv_t,
    text, text_p, acc_t, acc_i, coef_o, gte, gte_o, part, send_a, send_b, got_a, got_b,
    mid_a, mid_b, got_a2, got_b2, zin, got_z, fin,
    hop, hop_t, f_image, f_feat, f_proj, s_in, s_out, relay, joined, s_fwd, r_hop,
    s_img, r_img, s_txt, r_txt, s_py, r_py, r_pt, s_px, r_px, s_pc, r_pc,
    s_tf, r_tf, s_ge, r_ge, s_a, r_a, s_b, r_b, s_a2, r_a2, s_b2, r_b2,
    s_z, r_z, s_gz, r_gz, s_gx, r_gx, s_gy, r_gy,
):
    b, d, x, y, z, c = place()
    n_blk = lax.axis_size("blk")
    h, low = y // 2, lax.rem(y, 2)
    prev = (lax.rem(b + n_blk - 1, n_blk), d)
    nxt = (lax.rem(b + 1, n_blk), d)
    mate = device(x, y, z, 1 - c)
    xs = [lax.rem(x + o, NX) for o in range(NX)]
    ys = [lax.rem(y + o, NY) for o in range(NY)]
    zs = [lax.rem(z + o, NZ) for o in range(NZ)]
    to_x = [device(v, y, z, c) for v in xs]
    to_y = [device(x, v, z, c) for v in ys]
    to_z = [device(x, y, v, c) for v in zs]
    col = x * 2 + low
    before, after = lax.rem(col + 7, 8), lax.rem(col + 1, 8)
    to_before = device(before // 2, 2 * h + lax.rem(before, 2), z, c)
    to_after = device(after // 2, 2 * h + lax.rem(after, 2), z, c)

    def copy(src, dst, s, r, dev):
        return pltpu.make_async_remote_copy(
            src_ref=src, dst_ref=dst, send_sem=s, recv_sem=r, device_id=dev, device_id_type=MESH
        )

    def send(src, dst, s, r, dev):
        cp = copy(src, dst, s, r, dev)
        cp.start()
        return cp

    def all_sent(like, sem):
        copy(like, like, sem, sem, mate).wait_send()

    def all_here(like, sem):
        copy(like, like, sem, sem, mate).wait_recv()

    def rows16(start, size):
        return pl.ds(pl.multiple_of(start, 16), size)

    barrier = pltpu.get_barrier_semaphore()
    first, last = z == 0, z == NZ - 1
    partners = to_x[1:] + to_y[1:] + [mate, prev, to_z[NZ - 1], to_before, to_after]
    for dev in partners:
        pl.semaphore_signal(barrier, inc=1, device_id=dev, device_id_type=MESH)

    @pl.when(jnp.logical_not(last))
    def _():
        for dev in (nxt, to_z[1]):
            pl.semaphore_signal(barrier, inc=1, device_id=dev, device_id_type=MESH)

    mine = d * SH
    loads = [
        pltpu.make_async_copy(a, to, s_in.at[i])
        for i, (a, to) in enumerate(
            ((image_h, image), (feat_h, feat), (proj_h, full.at[rows16(mine, SH)]), (pos_h, pos))
        )
    ]
    for cp in loads:
        cp.start()

    @pl.when(first)
    def _():
        pl.semaphore_wait(barrier, len(partners))

    @pl.when(jnp.logical_not(first))
    def _():
        pl.semaphore_wait(barrier, len(partners) + 2)

    @pl.when(last)
    def _():
        pl.semaphore_signal(joined, inc=1, device_id=to_z[1], device_id_type=MESH)

    def pass_on(i):
        if i:
            pl.semaphore_wait(relay.at[i - 1], 2)
        if i < 5:
            for dev in (to_z[1], to_z[NZ - 1]):
                pl.semaphore_signal(relay.at[i], inc=1, device_id=dev, device_id_type=MESH)

    step = ROWS // IMG
    cut = lambda ref, i: ref.at[pl.ds(i * step, step)]
    c_img = [copy(cut(image_h, i), cut(image_n, i), s_img.at[0], r_img.at[i], prev) for i in range(IMG)]
    c_hop = [copy(cut(image_h, i), cut(hop, i), s_img.at[0], r_hop.at[i], to_before) for i in range(IMG)]
    c_fwd = [copy(cut(hop, i), cut(image_n, i), s_fwd.at[0], r_img.at[i], to_z[NZ - 1]) for i in range(IMG)]
    half = lambda ref, i: ref.at[pl.ds(i * (ROWS // 2), ROWS // 2)]
    c_txt = [copy(half(feat_h, i), half(feat_p, i), s_txt.at[0], r_txt.at[0], nxt) for i in range(2)]
    t_hop = copy(half(feat_h, 1), hop_t, s_txt.at[0], r_hop.at[IMG], to_after)
    t_fwd = copy(hop_t, half(feat_p, 1), s_fwd.at[1], r_txt.at[0], to_z[1])

    @pl.when(first)
    def _():
        for cp in c_hop:
            cp.start()

    @pl.when(jnp.logical_not(first))
    def _():
        for cp in c_img:
            cp.start()

    sign = 2 * low - 1
    xrow = x * PART
    rest = SH - NX * PART
    c_py, c_pt = [], []
    ahead = [device(x, lax.rem(y + sign * (k + 1) + NY, NY), z, c) for k in range(3)]
    for k in range(3):
        c_py.append(
            send(
                proj_h.at[rows16(xrow, PART)], full.at[rows16(mine + xrow, PART)],
                s_py.at[0], r_py.at[k], ahead[k],
            )
        )
    send(proj_h, full.at[rows16(mine, SH)], s_pc.at[0], r_pc.at[3], mate)
    for k in range(3):
        c_pt.append(
            send(
                proj_h.at[pl.ds(NX * PART, rest)], full.at[rows16(mine + NX * PART, rest)],
                s_py.at[0], r_pt.at[k], ahead[k],
            )
        )

    @pl.when(jnp.logical_not(last))
    def _():
        for cp in c_txt:
            cp.start()

    for cp in loads:
        cp.wait()
    turned = feat[...].T
    for i in range(8):
        tft[i % 2, i // 2] = turned[i * SH : (i + 1) * SH]
    c_tf = send(tft.at[1 - c], tft_o, s_tf.at[0], r_tf.at[0], mate)
    unit_rows(image, unit_in.at[pl.ds(0, ROWS)], inv_i)
    for i in range(NH):
        feat_k[i] = feat[:, i * 2 * SH : (i + 1) * 2 * SH]

    pairs, rows_of = [], []
    for way in (1, -2, 3):
        src_y = lax.rem(y + sign * way + NY, NY)
        pairs.append(src_y // 2)
        rows_of.append(((src_y // 2) * 2 + c) * SH)

    def to_mate(k, start, size):
        where = full.at[rows16(start, size)]
        send(where, where, s_pc.at[0], r_pc.at[k], mate)

    def mate_sent(k):
        all_here(full.at[pl.ds(0, SH)], r_pc.at[k])

    for k in range(3):
        c_py[k].wait_recv()
        where = full.at[rows16(rows_of[k] + xrow, PART)]
        for o in range(1, NX):
            send(where, where, s_px.at[0], r_px.at[k], to_x[o])
        to_mate(k, rows_of[k] + xrow, PART)

    @pl.when(first)
    def _():
        pl.semaphore_wait(joined, 1)
        for i in range(IMG):
            c_hop[i].wait_recv()
            c_fwd[i].start()

    pass_on(0)

    def add_text(pair, first):
        rhs_rows = rows16(pair * (2 * SH), 2 * SH)

        def cols_of(cols):
            v = nn_dot(feat_k[pair], full[rhs_rows, cols])
            text[:, cols] = v if first else text[:, cols] + v

        by_columns(cols_of)

    mate_sent(3)
    add_text(h, True)
    for k in range(3):
        all_here(full.at[pl.ds(0, (NX - 1) * PART)], r_px.at[k])
        for o in range(1, NX):
            to_mate(k, rows_of[k] + xs[NX - o] * PART, PART)
        c_pt[k].wait_recv()
        to_mate(k, rows_of[k] + NX * PART, rest)
        if k:
            mate_sent(k - 1)
            add_text(pairs[k - 1], False)

    @pl.when(last)
    def _():
        c_txt[0].start()
        t_hop.start()

    pass_on(1)
    for i in range(IMG):
        c_img[i].wait_recv()
        unit_rows(image_n.at[pl.ds(i * step, step)], unit_in.at[pl.ds(ROWS + i * step, step)], None)
    mate_sent(2)
    add_text(pairs[2], False)
    unit_t = unit_tp.at[pl.ds(0, ROWS)]
    unit_rows(text, unit_t, inv_t)
    factor = scale[0]
    offset = bias[0]

    logit = factor * nt_dot(unit_t[...], unit_in[...]) + offset
    hit = lax.broadcasted_iota(jnp.int32, (ROWS, ROWS), 0) == pos[...]
    label = jnp.where(hit, 1.0, -1.0).astype(F32)
    coef = (-label * sigmoid(-label * logit[:, :ROWS])).astype(BF)
    coef_o[...] = coef
    coef_all = jnp.concatenate([coef, sigmoid(logit[:, ROWS:]).astype(BF)], axis=1)

    def text_grads(cols):
        acc_t[:, cols] = nn_dot(coef_all, unit_in[:, cols])

    by_columns(text_grads)

    def share(i, rows):
        send(gte.at[rows], gte_o.at[rows], s_ge.at[0], r_ge.at[0], mate)

    norm_back(text, inv_t, acc_t, factor, gte, 64, share)
    pass_on(2)
    tft_c = tft[c].reshape(NH * SH, ROWS)

    def first_half(cols):
        part[:, cols] = nn_dot(tft_c, gte[:, cols])

    by_columns(first_half)
    c_tf.wait_recv()
    all_here(gte_o, r_ge.at[0])

    def group(i):
        return lax.rem(h + 1 + i, NH)

    def second_half(i):
        hh = group(i)
        both = (part[rows16(hh * SH, SH)] + nn_dot(tft_o[hh], gte_o[...])).astype(BF)
        for t in range(2 * NX * UN):
            l, xo, u = t // (NX * UN), (t // UN) % NX, t % UN
            if t < TILES:
                row, col = (t // 9) * 16, (t % 9) * 128
                tile = both[row : row + 16, col : col + 128]
            else:
                tile = jnp.zeros((16, 128), BF)
            if u < UA:
                send_a[xo, 2 * hh + l, u] = tile
            else:
                send_b[2 * hh + l, xo, u - UA] = tile

    def a_copy(i, o):
        two = pl.ds(2 * group(i), 2)
        return copy(send_a.at[xs[o], two], got_a.at[o - 1, two], s_a.at[0], r_a.at[i], to_x[o])

    def b_copy(to):
        return copy(send_b.at[to], got_b.at[y], s_b.at[0], r_b.at[0], device(x, to, z, c))

    def a2_copy(to):
        return copy(mid_a.at[to], got_a2.at[y], s_a2.at[0], r_a2.at[0], device(x, to, z, c))

    def start_group(i, _):
        second_half(i)
        for o in range(1, NX):
            a_copy(i, o).start()
        for l in range(2):
            b_copy(2 * group(i) + l).start()
        return 0

    twin = 2 * h + 1 - low
    lax.fori_loop(0, NH - 1, start_group, 0)
    second_half(NH - 1)
    for o in range(1, NX):
        a_copy(NH - 1, o).start()
    b_copy(twin).start()

    pass_on(3)

    @pl.when(last)
    def _():
        t_hop.wait_recv()
        t_fwd.start()

    def feat_cols(i, _):
        cols = pl.ds(pl.multiple_of(i * COLS, COLS), COLS)
        f_feat[:, cols] = nt_dot(gte[...], full[cols]).astype(BF)
        return 0

    lax.fori_loop(0, D // COLS, feat_cols, 0)
    out_feat = pltpu.make_async_copy(f_feat, g_feat, s_out.at[0])
    out_feat.start()

    def sum_a(i):
        all_here(got_a.at[:, pl.ds(2 * group(i), 2)], r_a.at[i])
        for l in range(2):
            at = 2 * group(i) + l
            v = send_a[x, at].astype(F32)
            for o in range(NX - 1):
                v = v + got_a[o, at].astype(F32)
            mid_a[at] = v.astype(BF)

    def a_group(i, _):
        sum_a(i)
        for l in range(2):
            a2_copy(2 * group(i) + l).start()
        return 0

    pass_on(4)
    lax.fori_loop(0, NH - 1, a_group, 0)
    sum_a(NH - 1)
    a2_copy(twin).start()

    all_here(got_b.at[pl.ds(0, NY - 1)], r_b.at[0])

    def sum_b(i, _):
        v = send_b[y, i].astype(F32)
        for o in range(1, NY):
            v = v + got_b[ys[o], i].astype(F32)
        mid_b[i] = v.astype(BF)
        return 0

    lax.fori_loop(0, NX, sum_b, 0)
    for o in range(1, NX):
        send(mid_b.at[xs[o]], got_b2.at[o - 1], s_b2.at[0], r_b2.at[0], to_x[o])

    all_here(got_a2.at[pl.ds(0, NY - 1)], r_a2.at[0])
    v = mid_a[y].astype(F32)
    for o in range(1, NY):
        v = v + got_a2[ys[o]].astype(F32)
    zin[0:UA] = v.astype(BF)
    all_here(got_b2, r_b2.at[0])
    v = mid_b[x].astype(F32)
    for o in range(NX - 1):
        v = v + got_b2[o].astype(F32)
    zin[UA:UN] = v.astype(BF)
    zin[UN] = jnp.zeros((16, 128), BF)

    pass_on(5)
    for o in range(1, NZ):
        send(zin.at[zs[o]], got_z.at[o - 1], s_z.at[0], r_z.at[0], to_z[o])
    all_here(got_z, r_z.at[0])
    v = zin[z].astype(F32)
    for o in range(NZ - 1):
        v = v + got_z[o].astype(F32)
    fin[low, x, z] = v.astype(BF)
    own = fin.at[low, x, z]
    for o in range(1, NZ):
        send(own, own, s_gz.at[0], r_gz.at[0], to_z[o])

    all_here(feat_p, r_txt.at[0])

    def text_p_cols(cols):
        text_p[:, cols] = nn_dot(feat_p[...], full[:, cols])

    by_columns(text_p_cols)
    unit_rows(text_p, unit_tp.at[pl.ds(ROWS, ROWS)], None)
    near_p = sigmoid(factor * nt_dot(unit_in[:ROWS], unit_tp[ROWS:]) + offset).astype(BF)
    coef_both = jnp.concatenate([coef_o[...].T, near_p], axis=1)

    def image_cols(cols):
        acc_i[:, cols] = nn_dot(coef_both, unit_tp[:, cols])

    by_columns(image_cols)
    norm_back(image, inv_i, acc_i, factor, f_image, 64)
    out_image = pltpu.make_async_copy(f_image, g_image, s_out.at[1])
    out_image.start()

    all_here(got_z, r_gz.at[0])
    own = fin.at[low, x, pl.ds(0, UN)]
    send(own, own, s_gy.at[0], r_gy.at[0], device(x, twin, z, c))
    c_gx = [send(own, own, s_gx.at[0], r_gx.at[o - 1], to_x[o]) for o in range(1, NX)]
    for o in (1, 3, 2):
        c_gx[o - 1].wait_recv()
        got = fin.at[low, xs[NX - o], pl.ds(0, UN)]
        send(got, got, s_gy.at[0], r_gy.at[0], device(x, twin, z, c))
    block = fin.at[low, :, pl.ds(0, UN)]
    all_here(block, r_gy.at[0])
    for t in range(TILES):
        l, xo, u = t // (NX * UN), (t // UN) % NX, t % UN
        row, col = (t // 9) * 16, (t % 9) * 128
        f_proj[row : row + 16, col : col + 128] = fin[l, xo, u]
    out_proj = pltpu.make_async_copy(f_proj, g_proj, s_out.at[2])
    out_proj.start()
    for like, sem in (
        (image, s_img), (feat, s_txt), (full.at[pl.ds(0, SH)], s_py), (tft_o, s_tf), (gte_o, s_ge),
        (full.at[pl.ds(0, 3 * (NX - 1) * PART)], s_px), (full.at[pl.ds(0, NH * SH)], s_pc),
        (got_a, s_a), (got_b.at[pl.ds(0, NY - 1)], s_b), (got_a2.at[pl.ds(0, NY - 1)], s_a2), (got_b2, s_b2),
        (got_z, s_z), (got_z, s_gz), (fin.at[low, pl.ds(0, NX - 1), pl.ds(0, UN)], s_gx), (block, s_gy),
    ):
        all_sent(like, sem.at[0])

    @pl.when(first)
    def _():
        all_sent(hop, s_fwd.at[0])

    @pl.when(last)
    def _():
        t_fwd.wait_send()

    for cp in (out_feat, out_image, out_proj):
        cp.wait()


def widen(*refs):
    srcs, dsts, narrow, wide, (s_in, s_out) = refs[:3], refs[3:6], refs[6:9], refs[9:12], refs[12:]
    pieces = [(a, r, 64) for a in range(2) for r in range(0, ROWS, 64)] + [(2, r, 48) for r in range(0, SH, 48)]
    ins, outs = [], []
    for i, (a, r, n) in enumerate(pieces):
        rows = pl.ds(r, n)
        ins.append(pltpu.make_async_copy(srcs[a].at[rows], narrow[a].at[rows], s_in.at[i]))
        outs.append(pltpu.make_async_copy(wide[a].at[rows], dsts[a].at[rows], s_out.at[i]))
        ins[-1].start()
    for i, (a, r, n) in enumerate(pieces):
        ins[i].wait()
        wide[a][r : r + n] = narrow[a][r : r + n].astype(F32)
        outs[i].start()
    for cp in outs:
        cp.wait()


def local(image_emb, text_feat, text_proj, pos_index, scale, bias):
    dma = lambda *into: sum(([pltpu.SemaphoreType.DMA((n,))] for n in (1,) + into), [])
    vm = pltpu.VMEM
    scratch = [
        vm((D, D), BF), vm((ROWS, D), BF), vm((ROWS, D), BF), vm((1, ROWS), jnp.int32),
        vm((ROWS, D), BF), vm((ROWS, D), BF), vm((NH, ROWS, 2 * SH), BF),
        vm((2, NH, SH, ROWS), BF), vm((NH, SH, ROWS), BF),
        vm((2 * ROWS, D), BF), vm((2 * ROWS, D), BF),
        vm((ROWS, 1), F32), vm((ROWS, 1), F32),
        vm((ROWS, D), F32), vm((ROWS, D), F32), vm((ROWS, D), F32), vm((ROWS, D), F32),
        vm((ROWS, ROWS), BF), vm((ROWS, D), BF), vm((ROWS, D), BF), vm((NH * SH, D), F32),
        vm((NX, NY, UA, 16, 128), BF), vm((NY, NX, UB, 16, 128), BF),
        vm((NX - 1, NY, UA, 16, 128), BF), vm((NY, NX, UB, 16, 128), BF),
        vm((NY, UA, 16, 128), BF), vm((NX, UB, 16, 128), BF),
        vm((NY, UA, 16, 128), BF), vm((NX - 1, UB, 16, 128), BF),
        vm((NZ, 16, 128), BF), vm((NZ - 1, 16, 128), BF), vm((2, NX, NZ, 16, 128), BF),
        vm((ROWS, D), BF),
        vm((ROWS // 2, D), BF), vm((ROWS, D), BF), vm((ROWS, D), BF), vm((SH, D), BF),
        pltpu.SemaphoreType.DMA((4,)), pltpu.SemaphoreType.DMA((3,)), pltpu.SemaphoreType.REGULAR((5,)), pltpu.SemaphoreType.REGULAR,
        pltpu.SemaphoreType.DMA((2,)), pltpu.SemaphoreType.DMA((IMG + 1,)),
    ]
    sems = (
        dma(IMG) + dma(1) + dma(3, 3) + dma(3) + dma(4) + dma(1) + dma(1)
        + dma(NH) + dma(1) + dma(1) + dma(1) + dma(1) + dma(1) + dma(NX - 1) + dma(1)
    )
    scalar = pl.BlockSpec(memory_space=pltpu.SMEM)
    far = pl.BlockSpec(memory_space=pltpu.HBM)
    g_image, g_feat, g_proj = pl.pallas_call(
        kernel,
        out_shape=(
            jax.ShapeDtypeStruct((ROWS, D), BF),
            jax.ShapeDtypeStruct((ROWS, D), BF),
            jax.ShapeDtypeStruct((SH, D), BF),
        ),
        in_specs=[far, far, far, far, scalar, scalar],
        out_specs=(far, far, far),
        scratch_shapes=scratch + sems,
        compiler_params=pltpu.CompilerParams(
            collective_id=0, has_side_effects=True, vmem_limit_bytes=58 * 1024 * 1024
        ),
        name="contrast_back",
    )(image_emb, text_feat, text_proj, pos_index, scale, bias)
    sizes = ((ROWS, D), (ROWS, D), (SH, D))
    return pl.pallas_call(
        widen,
        out_shape=tuple(jax.ShapeDtypeStruct(n, F32) for n in sizes),
        in_specs=[far] * 3,
        out_specs=(far,) * 3,
        scratch_shapes=[vm(n, BF) for n in sizes] + [vm(n, F32) for n in sizes]
        + [pltpu.SemaphoreType.DMA((11,)), pltpu.SemaphoreType.DMA((11,))],
        compiler_params=pltpu.CompilerParams(vmem_limit_bytes=58 * 1024 * 1024),
        name="widen",
    )(g_image, g_feat, g_proj)


def solution(mesh):
    return jax.shard_map(
        local,
        mesh=mesh,
        in_specs=(
            P(("blk", "dp"), None),
            P(("blk", "dp"), None),
            P("dp", None),
            P(("blk", "dp"), None),
            P(),
            P(),
        ),
        out_specs=(P(("blk", "dp"), None), P(("blk", "dp"), None), P("dp", None)),
        check_vma=False,
    )
```

```python
import jax
import jax.numpy as jnp
from jax import lax
from jax.experimental import pallas as pl
from jax.experimental.pallas import tpu as pltpu
from jax.sharding import PartitionSpec as P

MESH = pl.DeviceIdType.MESH
BF = jnp.bfloat16
F32 = jnp.float32
NX, NY, NZ, NH = 4, 8, 12, 4
ROWS, D, SH = 256, 1152, 144
PART = 32
UA, UB = 8, 3
UN = UA + UB
TILES = 81
COLS = 384
IMG = 4


def place():
    b, d = lax.axis_index("blk"), lax.axis_index("dp")
    x = b // (2 * NZ)
    low = lax.rem(b // NZ, 2)
    z = lax.rem(b, NZ)
    return b, d, x, (d // 2) * 2 + low, z, lax.rem(d, 2)


def device(x, y, z, c):
    return (x * (2 * NZ) + lax.rem(y, 2) * NZ + z, (y // 2) * 2 + c)


def nt_dot(a, b):
    return lax.dot_general(a, b, (((1,), (1,)), ((), ())), preferred_element_type=F32)


def nn_dot(a, b):
    return jnp.dot(a, b, preferred_element_type=F32)


def sigmoid(v):
    return 1.0 / (1.0 + jnp.exp(-v))


def inv_norm(v):
    return lax.rsqrt(jnp.sum(v * v, axis=-1, keepdims=True) + 1e-06)


def unit_rows(src, unit, inv, step=64):
    def body(i, _):
        rows = pl.ds(pl.multiple_of(i * step, step), step)
        v = src[rows].astype(F32)
        r = inv_norm(v)
        unit[rows] = (v * r).astype(BF)
        if inv is not None:
            inv[rows] = r
        return 0

    lax.fori_loop(0, src.shape[0] // step, body, 0)


def norm_back(src, inv, grad, factor, out, step, done=None):
    for i in range(src.shape[0] // step):
        rows = pl.ds(i * step, step)
        v, r, g = src[rows].astype(F32), inv[rows], factor * grad[rows]
        inner = jnp.sum(v * g, axis=-1, keepdims=True)
        out[rows] = (r * (g - v * (inner * r * r))).astype(out.dtype)
        if done is not None:
            done(i, rows)


def by_columns(fn):
    def body(i, _):
        fn(pl.ds(pl.multiple_of(i * COLS, COLS), COLS))
        return 0

    lax.fori_loop(0, D // COLS, body, 0)


def kernel(
    image_h, feat_h, proj_h, pos_h, scale, bias,
    g_image, g_feat, g_proj,
    full, image, feat, pos, image_n, feat_p, feat_k, tft, tft_o, unit_in, unit_tp, inv_i, inv_t,
    text, text_p, acc_t, acc_i, coef_o, gte, gte_o, part, send_a, send_b, got_a, got_b,
    mid_a, mid_b, got_a2, got_b2, zin, got_z, fin,
    hop, hop_t, f_image, f_feat, s_in, s_out, relay, joined, s_fwd, r_hop,
    s_img, r_img, s_txt, r_txt, s_py, r_py, r_pt, s_px, r_px, s_pc, r_pc,
    s_tf, r_tf, s_ge, r_ge, s_a, r_a, s_b, r_b, s_a2, r_a2, s_b2, r_b2,
    s_z, r_z, s_gz, r_gz, s_gx, r_gx, s_gy, r_gy,
):
    b, d, x, y, z, c = place()
    n_blk = lax.axis_size("blk")
    h, low = y // 2, lax.rem(y, 2)
    prev = (lax.rem(b + n_blk - 1, n_blk), d)
    nxt = (lax.rem(b + 1, n_blk), d)
    mate = device(x, y, z, 1 - c)
    xs = [lax.rem(x + o, NX) for o in range(NX)]
    ys = [lax.rem(y + o, NY) for o in range(NY)]
    zs = [lax.rem(z + o, NZ) for o in range(NZ)]
    to_x = [device(v, y, z, c) for v in xs]
    to_y = [device(x, v, z, c) for v in ys]
    to_z = [device(x, y, v, c) for v in zs]
    col = x * 2 + low
    before, after = lax.rem(col + 7, 8), lax.rem(col + 1, 8)
    to_before = device(before // 2, 2 * h + lax.rem(before, 2), z, c)
    to_after = device(after // 2, 2 * h + lax.rem(after, 2), z, c)

    def copy(src, dst, s, r, dev):
        return pltpu.make_async_remote_copy(
            src_ref=src, dst_ref=dst, send_sem=s, recv_sem=r, device_id=dev, device_id_type=MESH
        )

    def send(src, dst, s, r, dev):
        cp = copy(src, dst, s, r, dev)
        cp.start()
        return cp

    def all_sent(like, sem):
        copy(like, like, sem, sem, mate).wait_send()

    def all_here(like, sem):
        copy(like, like, sem, sem, mate).wait_recv()

    def rows16(start, size):
        return pl.ds(pl.multiple_of(start, 16), size)

    barrier = pltpu.get_barrier_semaphore()
    first, last = z == 0, z == NZ - 1
    partners = to_x[1:] + to_y[1:] + [mate, prev, to_z[NZ - 1], to_before, to_after]
    for dev in partners:
        pl.semaphore_signal(barrier, inc=1, device_id=dev, device_id_type=MESH)

    @pl.when(jnp.logical_not(last))
    def _():
        for dev in (nxt, to_z[1]):
            pl.semaphore_signal(barrier, inc=1, device_id=dev, device_id_type=MESH)

    mine = d * SH
    loads = [
        pltpu.make_async_copy(a, to, s_in.at[i])
        for i, (a, to) in enumerate(
            ((image_h, image), (feat_h, feat), (proj_h, full.at[rows16(mine, SH)]), (pos_h, pos))
        )
    ]
    for cp in loads:
        cp.start()

    @pl.when(first)
    def _():
        pl.semaphore_wait(barrier, len(partners))

    @pl.when(jnp.logical_not(first))
    def _():
        pl.semaphore_wait(barrier, len(partners) + 2)

    @pl.when(last)
    def _():
        pl.semaphore_signal(joined, inc=1, device_id=to_z[1], device_id_type=MESH)

    def pass_on(i):
        if i:
            pl.semaphore_wait(relay.at[i - 1], 2)
        if i < 5:
            for dev in (to_z[1], to_z[NZ - 1]):
                pl.semaphore_signal(relay.at[i], inc=1, device_id=dev, device_id_type=MESH)

    step = ROWS // IMG
    cut = lambda ref, i: ref.at[pl.ds(i * step, step)]
    c_img = [copy(cut(image_h, i), cut(image_n, i), s_img.at[0], r_img.at[i], prev) for i in range(IMG)]
    c_hop = [copy(cut(image_h, i), cut(hop, i), s_img.at[0], r_hop.at[i], to_before) for i in range(IMG)]
    c_fwd = [copy(cut(hop, i), cut(image_n, i), s_fwd.at[0], r_img.at[i], to_z[NZ - 1]) for i in range(IMG)]
    half = lambda ref, i: ref.at[pl.ds(i * (ROWS // 2), ROWS // 2)]
    c_txt = [copy(half(feat_h, i), half(feat_p, i), s_txt.at[0], r_txt.at[0], nxt) for i in range(2)]
    t_hop = copy(half(feat_h, 1), hop_t, s_txt.at[0], r_hop.at[IMG], to_after)
    t_fwd = copy(hop_t, half(feat_p, 1), s_fwd.at[1], r_txt.at[0], to_z[1])

    @pl.when(first)
    def _():
        for cp in c_hop:
            cp.start()

    @pl.when(jnp.logical_not(first))
    def _():
        for cp in c_img:
            cp.start()

    sign = 2 * low - 1
    xrow = x * PART
    rest = SH - NX * PART
    c_py, c_pt = [], []
    ahead = [device(x, lax.rem(y + sign * (k + 1) + NY, NY), z, c) for k in range(3)]
    for k in range(3):
        c_py.append(
            send(
                proj_h.at[rows16(xrow, PART)], full.at[rows16(mine + xrow, PART)],
                s_py.at[0], r_py.at[k], ahead[k],
            )
        )
    send(proj_h, full.at[rows16(mine, SH)], s_pc.at[0], r_pc.at[3], mate)
    for k in range(3):
        c_pt.append(
            send(
                proj_h.at[pl.ds(NX * PART, rest)], full.at[rows16(mine + NX * PART, rest)],
                s_py.at[0], r_pt.at[k], ahead[k],
            )
        )

    @pl.when(jnp.logical_not(last))
    def _():
        for cp in c_txt:
            cp.start()

    for cp in loads:
        cp.wait()
    turned = feat[...].T
    for i in range(8):
        tft[i % 2, i // 2] = turned[i * SH : (i + 1) * SH]
    c_tf = send(tft.at[1 - c], tft_o, s_tf.at[0], r_tf.at[0], mate)
    unit_rows(image, unit_in.at[pl.ds(0, ROWS)], inv_i)
    for i in range(NH):
        feat_k[i] = feat[:, i * 2 * SH : (i + 1) * 2 * SH]

    pairs, rows_of = [], []
    for way in (1, -2, 3):
        src_y = lax.rem(y + sign * way + NY, NY)
        pairs.append(src_y // 2)
        rows_of.append(((src_y // 2) * 2 + c) * SH)

    def to_mate(k, start, size):
        where = full.at[rows16(start, size)]
        send(where, where, s_pc.at[0], r_pc.at[k], mate)

    def mate_sent(k):
        all_here(full.at[pl.ds(0, SH)], r_pc.at[k])

    for k in range(3):
        c_py[k].wait_recv()
        where = full.at[rows16(rows_of[k] + xrow, PART)]
        for o in range(1, NX):
            send(where, where, s_px.at[0], r_px.at[k], to_x[o])
        to_mate(k, rows_of[k] + xrow, PART)

    @pl.when(first)
    def _():
        pl.semaphore_wait(joined, 1)
        for i in range(IMG):
            c_hop[i].wait_recv()
            c_fwd[i].start()

    pass_on(0)

    def add_text(pair, first):
        rhs_rows = rows16(pair * (2 * SH), 2 * SH)

        def cols_of(cols):
            v = nn_dot(feat_k[pair], full[rhs_rows, cols])
            text[:, cols] = v if first else text[:, cols] + v

        by_columns(cols_of)

    mate_sent(3)
    add_text(h, True)
    for k in range(3):
        all_here(full.at[pl.ds(0, (NX - 1) * PART)], r_px.at[k])
        for o in range(1, NX):
            to_mate(k, rows_of[k] + xs[NX - o] * PART, PART)
        c_pt[k].wait_recv()
        to_mate(k, rows_of[k] + NX * PART, rest)
        if k:
            mate_sent(k - 1)
            add_text(pairs[k - 1], False)

    @pl.when(last)
    def _():
        c_txt[0].start()
        t_hop.start()

    pass_on(1)
    for i in range(IMG):
        c_img[i].wait_recv()
        unit_rows(image_n.at[pl.ds(i * step, step)], unit_in.at[pl.ds(ROWS + i * step, step)], None)
    mate_sent(2)
    add_text(pairs[2], False)
    unit_t = unit_tp.at[pl.ds(0, ROWS)]
    unit_rows(text, unit_t, inv_t)
    factor = scale[0]
    offset = bias[0]

    logit = factor * nt_dot(unit_t[...], unit_in[...]) + offset
    hit = lax.broadcasted_iota(jnp.int32, (ROWS, ROWS), 0) == pos[...]
    label = jnp.where(hit, 1.0, -1.0).astype(F32)
    coef = (-label * sigmoid(-label * logit[:, :ROWS])).astype(BF)
    coef_o[...] = coef
    coef_all = jnp.concatenate([coef, sigmoid(logit[:, ROWS:]).astype(BF)], axis=1)

    def text_grads(cols):
        acc_t[:, cols] = nn_dot(coef_all, unit_in[:, cols])

    by_columns(text_grads)

    def share(i, rows):
        send(gte.at[rows], gte_o.at[rows], s_ge.at[0], r_ge.at[0], mate)

    norm_back(text, inv_t, acc_t, factor, gte, 64, share)
    pass_on(2)
    tft_c = tft[c].reshape(NH * SH, ROWS)

    def first_half(cols):
        part[:, cols] = nn_dot(tft_c, gte[:, cols])

    by_columns(first_half)
    c_tf.wait_recv()
    all_here(gte_o, r_ge.at[0])

    def group(i):
        return lax.rem(h + 1 + i, NH)

    def second_half(i):
        hh = group(i)
        both = (part[rows16(hh * SH, SH)] + nn_dot(tft_o[hh], gte_o[...])).astype(BF)
        for t in range(2 * NX * UN):
            l, xo, u = t // (NX * UN), (t // UN) % NX, t % UN
            if t < TILES:
                row, col = (t // 9) * 16, (t % 9) * 128
                tile = both[row : row + 16, col : col + 128]
            else:
                tile = jnp.zeros((16, 128), BF)
            if u < UA:
                send_a[xo, 2 * hh + l, u] = tile
            else:
                send_b[2 * hh + l, xo, u - UA] = tile

    def a_copy(i, o):
        two = pl.ds(2 * group(i), 2)
        return copy(send_a.at[xs[o], two], got_a.at[o - 1, two], s_a.at[0], r_a.at[i], to_x[o])

    def b_copy(to):
        return copy(send_b.at[to], got_b.at[y], s_b.at[0], r_b.at[0], device(x, to, z, c))

    def a2_copy(to):
        return copy(mid_a.at[to], got_a2.at[y], s_a2.at[0], r_a2.at[0], device(x, to, z, c))

    def start_group(i, _):
        second_half(i)
        for o in range(1, NX):
            a_copy(i, o).start()
        for l in range(2):
            b_copy(2 * group(i) + l).start()
        return 0

    twin = 2 * h + 1 - low
    lax.fori_loop(0, NH - 1, start_group, 0)
    second_half(NH - 1)
    for o in range(1, NX):
        a_copy(NH - 1, o).start()
    b_copy(twin).start()

    pass_on(3)

    @pl.when(last)
    def _():
        t_hop.wait_recv()
        t_fwd.start()

    def feat_cols(i, _):
        cols = pl.ds(pl.multiple_of(i * COLS, COLS), COLS)
        f_feat[:, cols] = nt_dot(gte[...], full[cols]).astype(BF)
        return 0

    lax.fori_loop(0, D // COLS, feat_cols, 0)
    out_feat = pltpu.make_async_copy(f_feat, g_feat, s_out.at[0])
    out_feat.start()

    def sum_a(i):
        all_here(got_a.at[:, pl.ds(2 * group(i), 2)], r_a.at[i])
        for l in range(2):
            at = 2 * group(i) + l
            v = send_a[x, at].astype(F32)
            for o in range(NX - 1):
                v = v + got_a[o, at].astype(F32)
            mid_a[at] = v.astype(BF)

    def a_group(i, _):
        sum_a(i)
        for l in range(2):
            a2_copy(2 * group(i) + l).start()
        return 0

    pass_on(4)
    lax.fori_loop(0, NH - 1, a_group, 0)
    sum_a(NH - 1)
    a2_copy(twin).start()

    all_here(got_b.at[pl.ds(0, NY - 1)], r_b.at[0])

    def sum_b(i, _):
        v = send_b[y, i].astype(F32)
        for o in range(1, NY):
            v = v + got_b[ys[o], i].astype(F32)
        mid_b[i] = v.astype(BF)
        return 0

    lax.fori_loop(0, NX, sum_b, 0)
    for o in range(1, NX):
        send(mid_b.at[xs[o]], got_b2.at[o - 1], s_b2.at[0], r_b2.at[0], to_x[o])

    all_here(got_a2.at[pl.ds(0, NY - 1)], r_a2.at[0])
    v = mid_a[y].astype(F32)
    for o in range(1, NY):
        v = v + got_a2[ys[o]].astype(F32)
    zin[0:UA] = v.astype(BF)
    all_here(got_b2, r_b2.at[0])
    v = mid_b[x].astype(F32)
    for o in range(NX - 1):
        v = v + got_b2[o].astype(F32)
    zin[UA:UN] = v.astype(BF)
    zin[UN] = jnp.zeros((16, 128), BF)

    pass_on(5)
    for o in range(1, NZ):
        send(zin.at[zs[o]], got_z.at[o - 1], s_z.at[0], r_z.at[0], to_z[o])
    all_here(got_z, r_z.at[0])
    v = zin[z].astype(F32)
    for o in range(NZ - 1):
        v = v + got_z[o].astype(F32)
    fin[low, x, z] = v.astype(BF)
    own = fin.at[low, x, z]
    for o in range(1, NZ):
        send(own, own, s_gz.at[0], r_gz.at[0], to_z[o])

    all_here(feat_p, r_txt.at[0])

    def text_p_cols(cols):
        text_p[:, cols] = nn_dot(feat_p[...], full[:, cols])

    by_columns(text_p_cols)
    unit_rows(text_p, unit_tp.at[pl.ds(ROWS, ROWS)], None)
    near_p = sigmoid(factor * nt_dot(unit_in[:ROWS], unit_tp[ROWS:]) + offset).astype(BF)
    coef_both = jnp.concatenate([coef_o[...].T, near_p], axis=1)

    def image_cols(cols):
        acc_i[:, cols] = nn_dot(coef_both, unit_tp[:, cols])

    by_columns(image_cols)
    norm_back(image, inv_i, acc_i, factor, f_image, 64)
    out_image = pltpu.make_async_copy(f_image, g_image, s_out.at[1])
    out_image.start()

    all_here(got_z, r_gz.at[0])
    own = fin.at[low, x, pl.ds(0, UN)]
    to_twin = device(x, twin, z, c)
    send(own, g_proj.at[low, x, pl.ds(0, UN)], s_gy.at[0], r_gy.at[0], to_twin)
    c_gx = [send(own, own, s_gx.at[0], r_gx.at[o - 1], to_x[o]) for o in range(1, NX)]
    for o in (1, 3, 2):
        c_gx[o - 1].wait_recv()
        at = xs[NX - o]
        send(fin.at[low, at, pl.ds(0, UN)], g_proj.at[low, at, pl.ds(0, UN)], s_gy.at[0], r_gy.at[0], to_twin)
    block = fin.at[low, :, pl.ds(0, UN)]
    out_proj = pltpu.make_async_copy(block, g_proj.at[low, :, pl.ds(0, UN)], s_out.at[2])
    out_proj.start()
    all_here(block, r_gy.at[0])
    for like, sem in (
        (image, s_img), (feat, s_txt), (full.at[pl.ds(0, SH)], s_py), (tft_o, s_tf), (gte_o, s_ge),
        (full.at[pl.ds(0, 3 * (NX - 1) * PART)], s_px), (full.at[pl.ds(0, NH * SH)], s_pc),
        (got_a, s_a), (got_b.at[pl.ds(0, NY - 1)], s_b), (got_a2.at[pl.ds(0, NY - 1)], s_a2), (got_b2, s_b2),
        (got_z, s_z), (got_z, s_gz), (fin.at[low, pl.ds(0, NX - 1), pl.ds(0, UN)], s_gx), (block, s_gy),
    ):
        all_sent(like, sem.at[0])

    @pl.when(first)
    def _():
        all_sent(hop, s_fwd.at[0])

    @pl.when(last)
    def _():
        t_fwd.wait_send()

    for cp in (out_feat, out_image, out_proj):
        cp.wait()


def widen(image, feat, tiles, g_image, g_feat, g_proj, n_image, n_feat, n_tiles, w_image, w_feat, w_proj, s_in, s_out):
    half = ROWS // 2
    get = lambda src, dst, i: pltpu.make_async_copy(src, dst, s_in.at[i])
    put = lambda src, dst, i: pltpu.make_async_copy(src, dst, s_out.at[i])
    pieces = [(a, pl.ds(r, half)) for a in range(2) for r in (0, half)]
    bf16, f32 = (n_image, n_feat), (w_image, w_feat)
    ins = [get((image, feat)[a].at[r], bf16[a].at[r], i) for i, (a, r) in enumerate(pieces)]
    outs = [put(f32[a].at[r], (g_image, g_feat)[a].at[r], i) for i, (a, r) in enumerate(pieces)]
    ins.append(get(tiles, n_tiles, 4))
    outs.append(put(w_proj, g_proj, 4))
    for cp in ins:
        cp.start()
    for i, (a, r) in enumerate(pieces):
        ins[i].wait()
        f32[a][r] = bf16[a][r].astype(F32)
        outs[i].start()
    ins[4].wait()
    for t in range(TILES):
        l, xo, u = t // (NX * UN), (t // UN) % NX, t % UN
        row, col = (t // 9) * 16, (t % 9) * 128
        w_proj[row : row + 16, col : col + 128] = n_tiles[l, xo, u].astype(F32)
    outs[4].start()
    for cp in outs:
        cp.wait()


def local(image_emb, text_feat, text_proj, pos_index, scale, bias):
    dma = lambda *into: sum(([pltpu.SemaphoreType.DMA((n,))] for n in (1,) + into), [])
    vm = pltpu.VMEM
    scratch = [
        vm((D, D), BF), vm((ROWS, D), BF), vm((ROWS, D), BF), vm((1, ROWS), jnp.int32),
        vm((ROWS, D), BF), vm((ROWS, D), BF), vm((NH, ROWS, 2 * SH), BF),
        vm((2, NH, SH, ROWS), BF), vm((NH, SH, ROWS), BF),
        vm((2 * ROWS, D), BF), vm((2 * ROWS, D), BF),
        vm((ROWS, 1), F32), vm((ROWS, 1), F32),
        vm((ROWS, D), F32), vm((ROWS, D), F32), vm((ROWS, D), F32), vm((ROWS, D), F32),
        vm((ROWS, ROWS), BF), vm((ROWS, D), BF), vm((ROWS, D), BF), vm((NH * SH, D), F32),
        vm((NX, NY, UA, 16, 128), BF), vm((NY, NX, UB, 16, 128), BF),
        vm((NX - 1, NY, UA, 16, 128), BF), vm((NY, NX, UB, 16, 128), BF),
        vm((NY, UA, 16, 128), BF), vm((NX, UB, 16, 128), BF),
        vm((NY, UA, 16, 128), BF), vm((NX - 1, UB, 16, 128), BF),
        vm((NZ, 16, 128), BF), vm((NZ - 1, 16, 128), BF), vm((2, NX, NZ, 16, 128), BF),
        vm((ROWS, D), BF),
        vm((ROWS // 2, D), BF), vm((ROWS, D), BF), vm((ROWS, D), BF),
        pltpu.SemaphoreType.DMA((4,)), pltpu.SemaphoreType.DMA((3,)), pltpu.SemaphoreType.REGULAR((5,)), pltpu.SemaphoreType.REGULAR,
        pltpu.SemaphoreType.DMA((2,)), pltpu.SemaphoreType.DMA((IMG + 1,)),
    ]
    sems = (
        dma(IMG) + dma(1) + dma(3, 3) + dma(3) + dma(4) + dma(1) + dma(1)
        + dma(NH) + dma(1) + dma(1) + dma(1) + dma(1) + dma(1) + dma(NX - 1) + dma(1)
    )
    scalar = pl.BlockSpec(memory_space=pltpu.SMEM)
    far = pl.BlockSpec(memory_space=pltpu.HBM)
    g_image, g_feat, g_proj = pl.pallas_call(
        kernel,
        out_shape=(
            jax.ShapeDtypeStruct((ROWS, D), BF),
            jax.ShapeDtypeStruct((ROWS, D), BF),
            jax.ShapeDtypeStruct((2, NX, NZ, 16, 128), BF),
        ),
        in_specs=[far, far, far, far, scalar, scalar],
        out_specs=(far, far, far),
        scratch_shapes=scratch + sems,
        compiler_params=pltpu.CompilerParams(
            collective_id=0, has_side_effects=True, vmem_limit_bytes=58 * 1024 * 1024
        ),
        name="contrast_back",
    )(image_emb, text_feat, text_proj, pos_index, scale, bias)
    sizes = ((ROWS, D), (ROWS, D), (SH, D))
    return pl.pallas_call(
        widen,
        out_shape=tuple(jax.ShapeDtypeStruct(n, F32) for n in sizes),
        in_specs=[far] * 3,
        out_specs=(far,) * 3,
        scratch_shapes=[vm(g.shape, BF) for g in (g_image, g_feat, g_proj)] + [vm(n, F32) for n in sizes]
        + [pltpu.SemaphoreType.DMA((5,)), pltpu.SemaphoreType.DMA((5,))],
        compiler_params=pltpu.CompilerParams(vmem_limit_bytes=58 * 1024 * 1024),
        name="widen",
    )(g_image, g_feat, g_proj)


def solution(mesh):
    return jax.shard_map(
        local,
        mesh=mesh,
        in_specs=(
            P(("blk", "dp"), None),
            P(("blk", "dp"), None),
            P("dp", None),
            P(("blk", "dp"), None),
            P(),
            P(),
        ),
        out_specs=(P(("blk", "dp"), None), P(("blk", "dp"), None), P("dp", None)),
        check_vma=False,
    )
```

```python
import jax
import jax.numpy as jnp
from jax import lax
from jax.experimental import pallas as pl
from jax.experimental.pallas import tpu as pltpu
from jax.sharding import PartitionSpec as P

MESH = pl.DeviceIdType.MESH
BF = jnp.bfloat16
F32 = jnp.float32
NX, NY, NZ, NH = 4, 8, 12, 4
ROWS, D, SH = 256, 1152, 144
PART = 32
UA, UB = 8, 3
UN = UA + UB
TILES = 81
COLS = 384
IMG = 4


def place():
    b, d = lax.axis_index("blk"), lax.axis_index("dp")
    x = b // (2 * NZ)
    low = lax.rem(b // NZ, 2)
    z = lax.rem(b, NZ)
    return b, d, x, (d // 2) * 2 + low, z, lax.rem(d, 2)


def device(x, y, z, c):
    return (x * (2 * NZ) + lax.rem(y, 2) * NZ + z, (y // 2) * 2 + c)


def nt_dot(a, b):
    return lax.dot_general(a, b, (((1,), (1,)), ((), ())), preferred_element_type=F32)


def nn_dot(a, b):
    return jnp.dot(a, b, preferred_element_type=F32)


def sigmoid(v):
    return 1.0 / (1.0 + jnp.exp(-v))


def inv_norm(v):
    return lax.rsqrt(jnp.sum(v * v, axis=-1, keepdims=True) + 1e-06)


def unit_rows(src, unit, inv, step=64):
    def body(i, _):
        rows = pl.ds(pl.multiple_of(i * step, step), step)
        v = src[rows].astype(F32)
        r = inv_norm(v)
        unit[rows] = (v * r).astype(BF)
        if inv is not None:
            inv[rows] = r
        return 0

    lax.fori_loop(0, src.shape[0] // step, body, 0)


def norm_back(src, inv, grad, factor, out, step, done=None):
    for i in range(src.shape[0] // step):
        rows = pl.ds(i * step, step)
        v, r, g = src[rows].astype(F32), inv[rows], factor * grad[rows]
        inner = jnp.sum(v * g, axis=-1, keepdims=True)
        out[rows] = (r * (g - v * (inner * r * r))).astype(out.dtype)
        if done is not None:
            done(i, rows)


def by_columns(fn):
    def body(i, _):
        fn(pl.ds(pl.multiple_of(i * COLS, COLS), COLS))
        return 0

    lax.fori_loop(0, D // COLS, body, 0)


def kernel(
    image_h, feat_h, proj_h, pos_h, scale, bias,
    g_image, g_feat, g_proj,
    full, image, feat, pos, image_n, feat_p, feat_k, tft, tft_o, unit_in, unit_tp, inv_i, inv_t,
    text, text_p, acc_t, acc_i, coef_o, gte, gte_o, part, send_a, send_b, got_a, got_b,
    mid_a, mid_b, got_a2, got_b2, zin, got_z, fin,
    hop, hop_t, f_image, f_feat, s_in, s_out, relay, joined, s_fwd, r_hop,
    s_img, r_img, s_txt, r_txt, s_py, r_py, r_pt, s_px, r_px, s_pc, r_pc,
    s_tf, r_tf, s_ge, r_ge, s_a, r_a, s_b, r_b, s_a2, r_a2, s_b2, r_b2,
    s_z, r_z, s_gz, r_gz, s_gx, r_gx, s_gy, r_gy,
):
    b, d, x, y, z, c = place()
    n_blk = lax.axis_size("blk")
    h, low = y // 2, lax.rem(y, 2)
    prev = (lax.rem(b + n_blk - 1, n_blk), d)
    nxt = (lax.rem(b + 1, n_blk), d)
    mate = device(x, y, z, 1 - c)
    xs = [lax.rem(x + o, NX) for o in range(NX)]
    ys = [lax.rem(y + o, NY) for o in range(NY)]
    zs = [lax.rem(z + o, NZ) for o in range(NZ)]
    to_x = [device(v, y, z, c) for v in xs]
    to_y = [device(x, v, z, c) for v in ys]
    to_z = [device(x, y, v, c) for v in zs]
    col = x * 2 + low
    before, after = lax.rem(col + 7, 8), lax.rem(col + 1, 8)
    to_before = device(before // 2, 2 * h + lax.rem(before, 2), z, c)
    to_after = device(after // 2, 2 * h + lax.rem(after, 2), z, c)

    def copy(src, dst, s, r, dev):
        return pltpu.make_async_remote_copy(
            src_ref=src, dst_ref=dst, send_sem=s, recv_sem=r, device_id=dev, device_id_type=MESH
        )

    def send(src, dst, s, r, dev):
        cp = copy(src, dst, s, r, dev)
        cp.start()
        return cp

    def all_sent(like, sem):
        copy(like, like, sem, sem, mate).wait_send()

    def all_here(like, sem):
        copy(like, like, sem, sem, mate).wait_recv()

    def rows16(start, size):
        return pl.ds(pl.multiple_of(start, 16), size)

    barrier = pltpu.get_barrier_semaphore()
    first, last = z == 0, z == NZ - 1
    partners = [to_y[o] for o in (4, 3, 5, 2, 6, 1, 7)] + [to_x[o] for o in (2, 1, 3)] + [mate, prev, to_z[NZ - 1], to_before, to_after]
    for dev in partners:
        pl.semaphore_signal(barrier, inc=1, device_id=dev, device_id_type=MESH)

    @pl.when(jnp.logical_not(last))
    def _():
        for dev in (nxt, to_z[1]):
            pl.semaphore_signal(barrier, inc=1, device_id=dev, device_id_type=MESH)

    mine = d * SH
    loads = [
        pltpu.make_async_copy(a, to, s_in.at[i])
        for i, (a, to) in enumerate(
            ((image_h, image), (feat_h, feat), (proj_h, full.at[rows16(mine, SH)]), (pos_h, pos))
        )
    ]
    for cp in loads:
        cp.start()

    @pl.when(first)
    def _():
        pl.semaphore_wait(barrier, len(partners))

    @pl.when(jnp.logical_not(first))
    def _():
        pl.semaphore_wait(barrier, len(partners) + 2)

    @pl.when(last)
    def _():
        pl.semaphore_signal(joined, inc=1, device_id=to_z[1], device_id_type=MESH)

    def pass_on(i):
        if i:
            pl.semaphore_wait(relay.at[i - 1], 2)
        if i < 5:
            for dev in (to_z[1], to_z[NZ - 1]):
                pl.semaphore_signal(relay.at[i], inc=1, device_id=dev, device_id_type=MESH)

    step = ROWS // IMG
    cut = lambda ref, i: ref.at[pl.ds(i * step, step)]
    c_img = [copy(cut(image_h, i), cut(image_n, i), s_img.at[0], r_img.at[i], prev) for i in range(IMG)]
    c_hop = [copy(cut(image_h, i), cut(hop, i), s_img.at[0], r_hop.at[i], to_before) for i in range(IMG)]
    c_fwd = [copy(cut(hop, i), cut(image_n, i), s_fwd.at[0], r_img.at[i], to_z[NZ - 1]) for i in range(IMG)]
    half = lambda ref, i: ref.at[pl.ds(i * (ROWS // 2), ROWS // 2)]
    c_txt = [copy(half(feat_h, i), half(feat_p, i), s_txt.at[0], r_txt.at[0], nxt) for i in range(2)]
    t_hop = copy(half(feat_h, 1), hop_t, s_txt.at[0], r_hop.at[IMG], to_after)
    t_fwd = copy(hop_t, half(feat_p, 1), s_fwd.at[1], r_txt.at[0], to_z[1])

    @pl.when(first)
    def _():
        for cp in c_hop:
            cp.start()

    @pl.when(jnp.logical_not(first))
    def _():
        for cp in c_img:
            cp.start()

    sign = 2 * low - 1
    xrow = x * PART
    rest = SH - NX * PART
    c_py, c_pt = [], []
    ahead = [device(x, lax.rem(y + sign * (k + 1) + NY, NY), z, c) for k in range(3)]
    for k in range(3):
        c_py.append(
            send(
                proj_h.at[rows16(xrow, PART)], full.at[rows16(mine + xrow, PART)],
                s_py.at[0], r_py.at[k], ahead[k],
            )
        )
    send(proj_h, full.at[rows16(mine, SH)], s_pc.at[0], r_pc.at[3], mate)
    for k in range(3):
        c_pt.append(
            send(
                proj_h.at[pl.ds(NX * PART, rest)], full.at[rows16(mine + NX * PART, rest)],
                s_py.at[0], r_pt.at[k], ahead[k],
            )
        )

    @pl.when(jnp.logical_not(last))
    def _():
        for cp in c_txt:
            cp.start()

    for cp in loads:
        cp.wait()
    turned = feat[...].T
    for i in range(8):
        tft[i % 2, i // 2] = turned[i * SH : (i + 1) * SH]
    c_tf = send(tft.at[1 - c], tft_o, s_tf.at[0], r_tf.at[0], mate)
    unit_rows(image, unit_in.at[pl.ds(0, ROWS)], inv_i)
    for i in range(NH):
        feat_k[i] = feat[:, i * 2 * SH : (i + 1) * 2 * SH]

    pairs, rows_of = [], []
    for way in (1, -2, 3):
        src_y = lax.rem(y + sign * way + NY, NY)
        pairs.append(src_y // 2)
        rows_of.append(((src_y // 2) * 2 + c) * SH)

    def to_mate(k, start, size):
        where = full.at[rows16(start, size)]
        send(where, where, s_pc.at[0], r_pc.at[k], mate)

    def mate_sent(k):
        all_here(full.at[pl.ds(0, SH)], r_pc.at[k])

    for k in range(3):
        c_py[k].wait_recv()
        where = full.at[rows16(rows_of[k] + xrow, PART)]
        for o in range(1, NX):
            send(where, where, s_px.at[0], r_px.at[k], to_x[o])
        to_mate(k, rows_of[k] + xrow, PART)

    @pl.when(first)
    def _():
        pl.semaphore_wait(joined, 1)
        for i in range(IMG):
            c_hop[i].wait_recv()
            c_fwd[i].start()

    pass_on(0)

    def add_text(pair, first):
        rhs_rows = rows16(pair * (2 * SH), 2 * SH)

        def cols_of(cols):
            v = nn_dot(feat_k[pair], full[rhs_rows, cols])
            text[:, cols] = v if first else text[:, cols] + v

        by_columns(cols_of)

    mate_sent(3)
    add_text(h, True)
    for k in range(3):
        all_here(full.at[pl.ds(0, (NX - 1) * PART)], r_px.at[k])
        for o in range(1, NX):
            to_mate(k, rows_of[k] + xs[NX - o] * PART, PART)
        c_pt[k].wait_recv()
        to_mate(k, rows_of[k] + NX * PART, rest)
        if k:
            mate_sent(k - 1)
            add_text(pairs[k - 1], False)

    @pl.when(last)
    def _():
        c_txt[0].start()
        t_hop.start()

    pass_on(1)
    for i in range(IMG):
        c_img[i].wait_recv()
        unit_rows(image_n.at[pl.ds(i * step, step)], unit_in.at[pl.ds(ROWS + i * step, step)], None)
    mate_sent(2)
    add_text(pairs[2], False)
    unit_t = unit_tp.at[pl.ds(0, ROWS)]
    unit_rows(text, unit_t, inv_t)
    factor = scale[0]
    offset = bias[0]

    logit = factor * nt_dot(unit_t[...], unit_in[...]) + offset
    hit = lax.broadcasted_iota(jnp.int32, (ROWS, ROWS), 0) == pos[...]
    label = jnp.where(hit, 1.0, -1.0).astype(F32)
    coef = (-label * sigmoid(-label * logit[:, :ROWS])).astype(BF)
    coef_o[...] = coef
    coef_all = jnp.concatenate([coef, sigmoid(logit[:, ROWS:]).astype(BF)], axis=1)

    def text_grads(cols):
        acc_t[:, cols] = nn_dot(coef_all, unit_in[:, cols])

    by_columns(text_grads)

    def share(i, rows):
        send(gte.at[rows], gte_o.at[rows], s_ge.at[0], r_ge.at[0], mate)

    norm_back(text, inv_t, acc_t, factor, gte, 64, share)
    pass_on(2)
    tft_c = tft[c].reshape(NH * SH, ROWS)

    def first_half(cols):
        part[:, cols] = nn_dot(tft_c, gte[:, cols])

    by_columns(first_half)
    c_tf.wait_recv()
    all_here(gte_o, r_ge.at[0])

    def group(i):
        return lax.rem(h + 1 + i, NH)

    def second_half(i):
        hh = group(i)
        both = (part[rows16(hh * SH, SH)] + nn_dot(tft_o[hh], gte_o[...])).astype(BF)
        for t in range(2 * NX * UN):
            l, xo, u = t // (NX * UN), (t // UN) % NX, t % UN
            if t < TILES:
                row, col = (t // 9) * 16, (t % 9) * 128
                tile = both[row : row + 16, col : col + 128]
            else:
                tile = jnp.zeros((16, 128), BF)
            if u < UA:
                send_a[xo, 2 * hh + l, u] = tile
            else:
                send_b[2 * hh + l, xo, u - UA] = tile

    def a_copy(i, o):
        two = pl.ds(2 * group(i), 2)
        return copy(send_a.at[xs[o], two], got_a.at[o - 1, two], s_a.at[0], r_a.at[i], to_x[o])

    def b_copy(to):
        return copy(send_b.at[to], got_b.at[y], s_b.at[0], r_b.at[0], device(x, to, z, c))

    def a2_copy(to):
        return copy(mid_a.at[to], got_a2.at[y], s_a2.at[0], r_a2.at[0], device(x, to, z, c))

    def start_group(i, _):
        second_half(i)
        for o in range(1, NX):
            a_copy(i, o).start()
        for l in range(2):
            b_copy(2 * group(i) + l).start()
        return 0

    twin = 2 * h + 1 - low
    lax.fori_loop(0, NH - 1, start_group, 0)
    second_half(NH - 1)
    for o in range(1, NX):
        a_copy(NH - 1, o).start()
    b_copy(twin).start()

    pass_on(3)

    @pl.when(last)
    def _():
        t_hop.wait_recv()
        t_fwd.start()

    def feat_cols(i, _):
        cols = pl.ds(pl.multiple_of(i * COLS, COLS), COLS)
        f_feat[:, cols] = nt_dot(gte[...], full[cols]).astype(BF)
        return 0

    lax.fori_loop(0, D // COLS, feat_cols, 0)
    out_feat = pltpu.make_async_copy(f_feat, g_feat, s_out.at[0])
    out_feat.start()

    def sum_a(i):
        all_here(got_a.at[:, pl.ds(2 * group(i), 2)], r_a.at[i])
        for l in range(2):
            at = 2 * group(i) + l
            v = send_a[x, at].astype(F32)
            for o in range(NX - 1):
                v = v + got_a[o, at].astype(F32)
            mid_a[at] = v.astype(BF)

    def a_group(i, _):
        sum_a(i)
        for l in range(2):
            a2_copy(2 * group(i) + l).start()
        return 0

    pass_on(4)
    lax.fori_loop(0, NH - 1, a_group, 0)
    sum_a(NH - 1)
    a2_copy(twin).start()

    all_here(got_b.at[pl.ds(0, NY - 1)], r_b.at[0])

    def sum_b(i, _):
        v = send_b[y, i].astype(F32)
        for o in range(1, NY):
            v = v + got_b[ys[o], i].astype(F32)
        mid_b[i] = v.astype(BF)
        return 0

    lax.fori_loop(0, NX, sum_b, 0)
    for o in range(1, NX):
        send(mid_b.at[xs[o]], got_b2.at[o - 1], s_b2.at[0], r_b2.at[0], to_x[o])

    all_here(got_a2.at[pl.ds(0, NY - 1)], r_a2.at[0])
    v = mid_a[y].astype(F32)
    for o in range(1, NY):
        v = v + got_a2[ys[o]].astype(F32)
    zin[0:UA] = v.astype(BF)
    all_here(got_b2, r_b2.at[0])
    v = mid_b[x].astype(F32)
    for o in range(NX - 1):
        v = v + got_b2[o].astype(F32)
    zin[UA:UN] = v.astype(BF)
    zin[UN] = jnp.zeros((16, 128), BF)

    pass_on(5)
    far_first = sorted(range(1, NZ), key=lambda o: -min(o, NZ - o))
    for o in far_first:
        send(zin.at[zs[o]], got_z.at[o - 1], s_z.at[0], r_z.at[0], to_z[o])
    all_here(got_z, r_z.at[0])
    v = zin[z].astype(F32)
    for o in range(NZ - 1):
        v = v + got_z[o].astype(F32)
    fin[low, x, z] = v.astype(BF)
    own = fin.at[low, x, z]
    for o in far_first:
        send(own, own, s_gz.at[0], r_gz.at[0], to_z[o])

    all_here(feat_p, r_txt.at[0])

    def text_p_cols(cols):
        text_p[:, cols] = nn_dot(feat_p[...], full[:, cols])

    by_columns(text_p_cols)
    unit_rows(text_p, unit_tp.at[pl.ds(ROWS, ROWS)], None)
    near_p = sigmoid(factor * nt_dot(unit_in[:ROWS], unit_tp[ROWS:]) + offset).astype(BF)
    coef_both = jnp.concatenate([coef_o[...].T, near_p], axis=1)

    def image_cols(cols):
        acc_i[:, cols] = nn_dot(coef_both, unit_tp[:, cols])

    by_columns(image_cols)
    norm_back(image, inv_i, acc_i, factor, f_image, 64)
    out_image = pltpu.make_async_copy(f_image, g_image, s_out.at[1])
    out_image.start()

    all_here(got_z, r_gz.at[0])
    own = fin.at[low, x, pl.ds(0, UN)]
    to_twin = device(x, twin, z, c)
    send(own, g_proj.at[low, x, pl.ds(0, UN)], s_gy.at[0], r_gy.at[0], to_twin)
    c_gx = [send(own, own, s_gx.at[0], r_gx.at[o - 1], to_x[o]) for o in range(1, NX)]
    for o in (1, 3, 2):
        c_gx[o - 1].wait_recv()
        at = xs[NX - o]
        send(fin.at[low, at, pl.ds(0, UN)], g_proj.at[low, at, pl.ds(0, UN)], s_gy.at[0], r_gy.at[0], to_twin)
    block = fin.at[low, :, pl.ds(0, UN)]
    out_proj = pltpu.make_async_copy(block, g_proj.at[low, :, pl.ds(0, UN)], s_out.at[2])
    out_proj.start()
    all_here(block, r_gy.at[0])
    for like, sem in (
        (image, s_img), (feat, s_txt), (full.at[pl.ds(0, SH)], s_py), (tft_o, s_tf), (gte_o, s_ge),
        (full.at[pl.ds(0, 3 * (NX - 1) * PART)], s_px), (full.at[pl.ds(0, NH * SH)], s_pc),
        (got_a, s_a), (got_b.at[pl.ds(0, NY - 1)], s_b), (got_a2.at[pl.ds(0, NY - 1)], s_a2), (got_b2, s_b2),
        (got_z, s_z), (got_z, s_gz), (fin.at[low, pl.ds(0, NX - 1), pl.ds(0, UN)], s_gx), (block, s_gy),
    ):
        all_sent(like, sem.at[0])

    @pl.when(first)
    def _():
        all_sent(hop, s_fwd.at[0])

    @pl.when(last)
    def _():
        t_fwd.wait_send()

    for cp in (out_feat, out_image, out_proj):
        cp.wait()


def widen(image, feat, tiles, g_image, g_feat, g_proj, n_image, n_feat, n_tiles, w_image, w_feat, w_proj, s_in, s_out):
    half = ROWS // 2
    get = lambda src, dst, i: pltpu.make_async_copy(src, dst, s_in.at[i])
    put = lambda src, dst, i: pltpu.make_async_copy(src, dst, s_out.at[i])
    pieces = [(a, pl.ds(r, half)) for a in range(2) for r in (0, half)]
    bf16, f32 = (n_image, n_feat), (w_image, w_feat)
    ins = [get((image, feat)[a].at[r], bf16[a].at[r], i) for i, (a, r) in enumerate(pieces)]
    outs = [put(f32[a].at[r], (g_image, g_feat)[a].at[r], i) for i, (a, r) in enumerate(pieces)]
    ins.append(get(tiles, n_tiles, 4))
    outs.append(put(w_proj, g_proj, 4))
    for cp in ins:
        cp.start()
    for i, (a, r) in enumerate(pieces):
        ins[i].wait()
        f32[a][r] = bf16[a][r].astype(F32)
        outs[i].start()
    ins[4].wait()
    for t in range(TILES):
        l, xo, u = t // (NX * UN), (t // UN) % NX, t % UN
        row, col = (t // 9) * 16, (t % 9) * 128
        w_proj[row : row + 16, col : col + 128] = n_tiles[l, xo, u].astype(F32)
    outs[4].start()
    for cp in outs:
        cp.wait()


def local(image_emb, text_feat, text_proj, pos_index, scale, bias):
    dma = lambda *into: sum(([pltpu.SemaphoreType.DMA((n,))] for n in (1,) + into), [])
    vm = pltpu.VMEM
    scratch = [
        vm((D, D), BF), vm((ROWS, D), BF), vm((ROWS, D), BF), vm((1, ROWS), jnp.int32),
        vm((ROWS, D), BF), vm((ROWS, D), BF), vm((NH, ROWS, 2 * SH), BF),
        vm((2, NH, SH, ROWS), BF), vm((NH, SH, ROWS), BF),
        vm((2 * ROWS, D), BF), vm((2 * ROWS, D), BF),
        vm((ROWS, 1), F32), vm((ROWS, 1), F32),
        vm((ROWS, D), F32), vm((ROWS, D), F32), vm((ROWS, D), F32), vm((ROWS, D), F32),
        vm((ROWS, ROWS), BF), vm((ROWS, D), BF), vm((ROWS, D), BF), vm((NH * SH, D), F32),
        vm((NX, NY, UA, 16, 128), BF), vm((NY, NX, UB, 16, 128), BF),
        vm((NX - 1, NY, UA, 16, 128), BF), vm((NY, NX, UB, 16, 128), BF),
        vm((NY, UA, 16, 128), BF), vm((NX, UB, 16, 128), BF),
        vm((NY, UA, 16, 128), BF), vm((NX - 1, UB, 16, 128), BF),
        vm((NZ, 16, 128), BF), vm((NZ - 1, 16, 128), BF), vm((2, NX, NZ, 16, 128), BF),
        vm((ROWS, D), BF),
        vm((ROWS // 2, D), BF), vm((ROWS, D), BF), vm((ROWS, D), BF),
        pltpu.SemaphoreType.DMA((4,)), pltpu.SemaphoreType.DMA((3,)), pltpu.SemaphoreType.REGULAR((5,)), pltpu.SemaphoreType.REGULAR,
        pltpu.SemaphoreType.DMA((2,)), pltpu.SemaphoreType.DMA((IMG + 1,)),
    ]
    sems = (
        dma(IMG) + dma(1) + dma(3, 3) + dma(3) + dma(4) + dma(1) + dma(1)
        + dma(NH) + dma(1) + dma(1) + dma(1) + dma(1) + dma(1) + dma(NX - 1) + dma(1)
    )
    scalar = pl.BlockSpec(memory_space=pltpu.SMEM)
    far = pl.BlockSpec(memory_space=pltpu.HBM)
    g_image, g_feat, g_proj = pl.pallas_call(
        kernel,
        out_shape=(
            jax.ShapeDtypeStruct((ROWS, D), BF),
            jax.ShapeDtypeStruct((ROWS, D), BF),
            jax.ShapeDtypeStruct((2, NX, NZ, 16, 128), BF),
        ),
        in_specs=[far, far, far, far, scalar, scalar],
        out_specs=(far, far, far),
        scratch_shapes=scratch + sems,
        compiler_params=pltpu.CompilerParams(
            collective_id=0, has_side_effects=True, vmem_limit_bytes=58 * 1024 * 1024
        ),
        name="contrast_back",
    )(image_emb, text_feat, text_proj, pos_index, scale, bias)
    sizes = ((ROWS, D), (ROWS, D), (SH, D))
    return pl.pallas_call(
        widen,
        out_shape=tuple(jax.ShapeDtypeStruct(n, F32) for n in sizes),
        in_specs=[far] * 3,
        out_specs=(far,) * 3,
        scratch_shapes=[vm(g.shape, BF) for g in (g_image, g_feat, g_proj)] + [vm(n, F32) for n in sizes]
        + [pltpu.SemaphoreType.DMA((5,)), pltpu.SemaphoreType.DMA((5,))],
        compiler_params=pltpu.CompilerParams(vmem_limit_bytes=58 * 1024 * 1024),
        name="widen",
    )(g_image, g_feat, g_proj)


def solution(mesh):
    return jax.shard_map(
        local,
        mesh=mesh,
        in_specs=(
            P(("blk", "dp"), None),
            P(("blk", "dp"), None),
            P("dp", None),
            P(("blk", "dp"), None),
            P(),
            P(),
        ),
        out_specs=(P(("blk", "dp"), None), P(("blk", "dp"), None), P("dp", None)),
        check_vma=False,
    )
```
